256 devices in a mesh: gx: 32 (over z, x_hi, core), gy: 8 (over x_lo, y).
Axes of the slice: x: 4 (x_hi: 2, x_lo: 2; x = x_hi * 2 + x_lo), y: 4, z: 8, core: 2. Of those that a mesh axis runs over, the one named last changes fastest.
Arguments:
- head_start: float32 [256, 128, 128], P('gx', 'gy'), may hold values from -6 to 6
- solute_start: float32 [256, 128, 128], P('gx', 'gy'), may hold values from -6 to 6
- source: float32 [256, 128, 128], P('gx', 'gy'), may hold values from -3 to 3
- log_conductivity: float32 [256, 128, 128], P('gx', 'gy'), may hold values from -1 to 1
- dispersivity: float32 [256, 128, 128], P('gx', 'gy'), may hold values from 0.2 to 2
- material: int32 [256, 128, 128], P('gx', 'gy'), may hold values from 0 to 7
- material_table: float32 [8], replicated, may hold values from 0.3 to 3
- boundary: int32 [256, 128], P('gx', 'gy'), may hold values from 0 to 2
- head_weight: float32 [256, 128, 128], P('gx', 'gy'), may hold values from -6 to 6
- solute_weight: float32 [256, 128, 128], P('gx', 'gy'), may hold values from -6 to 6
Outputs:
- head_final: float32 [256, 128, 128], P('gx', 'gy')
- solute_final: float32 [256, 128, 128], P('gx', 'gy')
- grad_conductivity: float32 [256, 128, 128], P('gx', 'gy')
- grad_dispersivity: float32 [256, 128, 128], P('gx', 'gy')
- grad_table: float32 [8], replicated
The draws below stay inside these ranges and needn't reach their ends.
All inputs are finite; a program needn't handle non-finite values.
Results may differ from the reference program's by a relative error of at most 0.0003.
Values sent between devices are 32-bit elements; how exact they have to be, the bound alone decides.
A program may use at most 128 MiB of HBM per device.

```python
import math
import jax
import jax.numpy as jnp

NZ = 128
STEPS = 2
SWEEPS = 8
MATS = 8
NX = 256
NY = 128


def touch_ends(drawn, key, low, high):
    place = [jax.random.randint(jax.random.fold_in(key, axis), (), 0, length) for axis, length in enumerate(drawn.shape)]
    widest = drawn.shape.index(max(drawn.shape))
    next_to = place[:widest] + [(place[widest] + 1) % drawn.shape[widest]] + place[widest + 1:]
    return drawn.at[tuple(place)].set(low).at[tuple(next_to)].set(high)


def level_of(stream_key, shape, pieces, smallest, top_value):
    level, own = 1.0, jax.random.fold_in(stream_key, 6)
    for position, parts in pieces:
        steps = jnp.exp(jax.random.uniform(jax.random.fold_in(own, position), (parts,), jnp.float32, smallest / len(pieces), top_value / len(pieces)))
        level = level * jnp.repeat(steps, shape[position] // parts).reshape([-1 if axis == position else 1 for axis in range(len(shape))])
    return level


def centred(stream_key, extent, spread, limit, cuts=(), dtype=jnp.bfloat16):
    array = spread * jax.random.normal(stream_key, extent, jnp.float32)
    if cuts:
        array = array * level_of(stream_key, extent, cuts, -0.22, 0.18)
    return jnp.clip(array, -limit, limit).astype(dtype)


def setup_inputs(seed: int = 0) -> dict:
    seeds = jax.random.split(jax.random.key(seed), 11)
    head_start = centred(seeds[0], (NX, NY, NZ), 1.0, 6.0, ((0, 32), (1, 8)), jnp.float32)
    solute_start = centred(seeds[1], (NX, NY, NZ), 1.0, 6.0, ((0, 32), (1, 8)), jnp.float32)
    source = centred(seeds[2], (NX, NY, NZ), 0.5, 3.0, ((0, 32), (1, 8)), jnp.float32)
    log_conductivity = jnp.clip(jax.random.uniform(seeds[3], (NX, NY, NZ), jnp.float32, -1.0, 1.0) * level_of(seeds[3], (NX, NY, NZ), ((0, 32), (1, 8)), -0.4, 0.0), -1.0, 1.0)
    dispersivity = jnp.clip(jnp.exp(math.log(2.0) - 2.3025851 * jax.random.uniform(seeds[4], (NX, NY, NZ), jnp.float32) ** level_of(seeds[4], (NX, NY, NZ), ((0, 32), (1, 8)), -0.2, 0.2)), 0.2, 2.0)
    material = touch_ends(jax.random.randint(seeds[5], (NX, NY, NZ), 0, MATS), jax.random.fold_in(seeds[5], 1), 0, MATS - 1).astype(jnp.int32)
    material_table = jnp.clip(jnp.exp(jax.random.uniform(seeds[6], (MATS,), jnp.float32, math.log(0.3), math.log(3.0))), 0.3, 3.0)
    boundary = touch_ends(jax.random.randint(seeds[7], (NX, NY), 0, 3), jax.random.fold_in(seeds[7], 1), 0, 2).astype(jnp.int32)
    head_weight = centred(seeds[8], (NX, NY, NZ), 1.0, 6.0, ((0, 32), (1, 8)), jnp.float32)
    solute_weight = centred(seeds[9], (NX, NY, NZ), 1.0, 6.0, ((0, 32), (1, 8)), jnp.float32)
    return {"head_start": head_start, "solute_start": solute_start, "source": source, "log_conductivity": log_conductivity, "dispersivity": dispersivity, "material": material, "material_table": material_table, "boundary": boundary, "head_weight": head_weight, "solute_weight": solute_weight}


coupling_rate = 0.5

def coefficients(values, top_factor):
    half_rows = 0.5 * (values[:-1] + values[1:])
    half_cols = 0.5 * (values[:, :-1] + values[:, 1:])
    half_layers = 0.5 * (values[:, :, :-1] + values[:, :, 1:])
    east_side = jnp.pad(half_rows, ((0, 1), (0, 0), (0, 0)))
    west_side = jnp.pad(half_rows, ((1, 0), (0, 0), (0, 0)))
    north_side = jnp.pad(half_cols, ((0, 0), (0, 1), (0, 0)))
    south_side = jnp.pad(half_cols, ((0, 0), (1, 0), (0, 0)))
    upper_side = jnp.pad(half_layers, ((0, 0), (0, 0), (0, 1)))
    lower_side = jnp.pad(half_layers, ((0, 0), (0, 0), (1, 0)))
    top_term = jnp.zeros_like(values).at[:, :, -1].set(top_factor * values[:, :, -1])
    diagonal = 1.0 + east_side + west_side + north_side + south_side + upper_side + lower_side + top_term
    return ((east_side, west_side, north_side, south_side, upper_side, lower_side), diagonal)

def neighbours(current, weights):
    padded = jnp.pad(current, 1)
    total = weights[0] * padded[2:, 1:-1, 1:-1] + weights[1] * padded[:-2, 1:-1, 1:-1]
    total = total + weights[2] * padded[1:-1, 2:, 1:-1] + weights[3] * padded[1:-1, :-2, 1:-1]
    total = total + weights[4] * padded[1:-1, 1:-1, 2:] + weights[5] * padded[1:-1, 1:-1, :-2]
    return total

def relax_field(values, top_factor, start, right_side):
    weights, diagonal = coefficients(values, top_factor)
    current = start
    for sweep_index in range(SWEEPS):
        current = (right_side + neighbours(current, weights)) / diagonal
    return current

def advance(states, conductivity, spreading, top_factor, source):
    head, solute = states
    head = relax_field(conductivity, top_factor, head, head + source)
    solute = relax_field(spreading, top_factor, solute, solute + coupling_rate * head)
    return (head, solute)

def forward_window(log_values, spread_values, table_values, head_start, solute_start, source, material, top_factor):
    conductivity = table_values[material] * jnp.exp(log_values)
    spreading = spread_values * conductivity
    advance_step = jax.checkpoint(advance)
    states = (head_start, solute_start)
    for step_index in range(STEPS):
        states = advance_step(states, conductivity, spreading, top_factor, source)
    return states

def reference(head_start, solute_start, source, log_conductivity, dispersivity, material, material_table, boundary, head_weight, solute_weight):
    top_factor = jnp.where(boundary == 1, 1.0, jnp.where(boundary == 2, 4.0, 0.0)).astype(jnp.float32)

    def window(log_values, spread_values, table_values):
        return forward_window(log_values, spread_values, table_values, head_start, solute_start, source, material, top_factor)
    finals, pullback = jax.vjp(window, log_conductivity, dispersivity, material_table)
    grads = pullback((head_weight, solute_weight))
    return (finals[0], finals[1], grads[0], grads[1], grads[2])
```

```python
import jax
import jax.numpy as jnp
from jax import lax
from jax.experimental import pallas as pl
from jax.experimental.pallas import tpu as pltpu
from jax.sharding import PartitionSpec as P

SWEEPS = 8
MATS = 8
coupling_rate = 0.5

BX, BY, NZ, HALO = 8, 16, 128, 8
GX, GY = 32, 8
ROWS = BX + 2 * HALO
COLS = BY + 2 * HALO
PAD = COLS + 16
Y0, Y1 = 8, 8 + COLS
OX, OY = HALO, 8 + HALO
MESH = pl.DeviceIdType.MESH
DIRS = ((1, 0), (-1, 0), (0, 1), (0, -1), (1, 1), (1, -1), (-1, 1), (-1, -1))
HEAD, SOLUTE = 0, 1


def place(lx, ly):
    return (lax.rem(lx + GX, GX), lax.rem(ly + GY, GY))


def x_part(dx):
    return {0: slice(OX, OX + BX), 1: slice(0, HALO), -1: slice(OX + BX, ROWS)}[dx]


def y_from(dy):
    return {0: (0, BY), 1: (BY - HALO, HALO), -1: (0, HALO)}[dy]


def y_into(dy):
    return {0: (HALO, BY), 1: (0, HALO), -1: (HALO + BY, HALO)}[dy]


def up(cells):
    return pltpu.roll(cells, NZ - 1, 1)


def down(cells):
    return pltpu.roll(cells, 1, 1)


def kernel(
    head_in,
    solute_in,
    source_in,
    log_in,
    disp_in,
    material_in,
    table_in,
    boundary_in,
    head_weight_in,
    solute_weight_in,
    head_out,
    solute_out,
    grad_cond_out,
    grad_disp_out,
    grad_table_out,
    first,
    second,
    cx,
    cy,
    czu,
    czd,
    inv,
    rhs,
    xe_head,
    xo_head,
    xe_solute,
    xo_solute,
    lam_even,
    lam_odd,
    acc_side,
    acc_layer,
    acc_drop,
    part_a,
    part_b,
    send_sem,
    recv_sem,
    send_a,
    recv_a,
    send_b,
    recv_b,
):
    gx, gy = lax.axis_index("gx"), lax.axis_index("gy")
    lx, ly = gx, gy
    neighbours = {d: place(lx + d[0], ly + d[1]) for d in DIRS}
    z_at, hi_at, core_at = gx // 4, lax.rem(gx // 2, 2), lax.rem(gx, 2)
    a_at = hi_at * 8 + gy
    b_at = z_at * 2 + core_at

    def a_device(t):
        to = lax.rem(a_at + t, 16)
        return (z_at * 4 + (to // 8) * 2 + core_at, lax.rem(to, 8))

    def b_device(t):
        to = lax.rem(b_at + t, 16)
        return ((to // 2) * 4 + hi_at * 2 + lax.rem(to, 2), gy)

    barrier = pltpu.get_barrier_semaphore()
    for d in DIRS:
        pl.semaphore_signal(barrier, inc=1, device_id=neighbours[d], device_id_type=MESH)
    for t in range(1, 16):
        pl.semaphore_signal(barrier, inc=1, device_id=a_device(t), device_id_type=MESH)
        pl.semaphore_signal(barrier, inc=1, device_id=b_device(t), device_id_type=MESH)

    lane = lax.broadcasted_iota(jnp.int32, (COLS, NZ), 1)
    col = lax.broadcasted_iota(jnp.int32, (COLS, NZ), 0) + (ly * BY - HALO)
    col_in = jnp.where((col >= 0) & (col < GY * BY), 1.0, 0.0)
    col_face = jnp.where((col >= 0) & (col + 1 < GY * BY), 0.5, 0.0)
    top_lane = lane == NZ - 1

    def row_in(i):
        at = lx * BX + (i - HALO)
        return jnp.where((at >= 0) & (at < GX * BX), 1.0, 0.0)

    own = slice(HALO, HALO + BY)
    for r in range(BX):
        material = material_in[r]
        base = jnp.zeros((BY, NZ), jnp.float32)
        for m in range(MATS):
            base = jnp.where(material == m, table_in[m], base)
        conductivity = base * jnp.exp(log_in[r])
        first[1, r, own, :] = conductivity
        first[1, BX + r, own, :] = head_in[r]
        first[1, 2 * BX + r, own, :] = source_in[r]
        second[1, r, own, :] = disp_in[r] * conductivity
        second[1, BX + r, own, :] = solute_in[r]
    kind = boundary_in[...]
    factor = jnp.where(kind == 1, 1.0, jnp.where(kind == 2, 4.0, 0.0)).astype(jnp.float32)
    diagonal_at = lax.broadcasted_iota(jnp.int32, (BY, BY), 0) == lax.broadcasted_iota(
        jnp.int32, (BY, BY), 1
    )
    tops = jnp.zeros((BY, NZ), jnp.float32)
    for r in range(BX):
        spread = jnp.broadcast_to(factor[r : r + 1, :], (BY, BY))
        column = jnp.sum(jnp.where(diagonal_at, spread, 0.0), axis=1, keepdims=True)
        tops = jnp.where(lane[:BY] == r, column, tops)
    first[1, 3 * BX, own, :] = tops

    pl.semaphore_wait(barrier, len(DIRS) + 30)

    def exchange(event, source_of, target_of, dirs=DIRS):
        copies = []
        for d in dirs:
            k = DIRS.index(d)
            copy = pltpu.make_async_remote_copy(
                src_ref=source_of(d),
                dst_ref=target_of(d),
                send_sem=send_sem.at[event, k],
                recv_sem=recv_sem.at[event, k],
                device_id=neighbours[d],
                device_id_type=MESH,
            )
            copy.start()
            copies.append(copy)
        return copies

    def exchange_pack(event, pack):
        def source_of(d):
            start, size = y_from(d[1])
            return pack.at[1, :, pl.ds(HALO + start, size), :]

        def target_of(d):
            start, size = y_into(d[1])
            return pack.at[1 - d[0], :, pl.ds(start, size), :]

        return exchange(event, source_of, target_of)

    def exchange_field(event, ref, *lead, dirs=DIRS):
        def source_of(d):
            start, size = y_from(d[1])
            return ref.at[(*lead, pl.ds(OX, BX), pl.ds(OY + start, size), slice(None))]

        def target_of(d):
            start, size = y_into(d[1])
            part = x_part(d[0])
            return ref.at[
                (*lead, pl.ds(part.start, part.stop - part.start), pl.ds(Y0 + start, size), slice(None))
            ]

        return exchange(event, source_of, target_of, dirs)

    def arrive(copies):
        for copy in copies:
            copy.wait_recv()

    started = []
    got_first = exchange_pack(0, first)
    got_second = exchange_pack(1, second)
    started += got_first + got_second

    own_y = pl.ds(OY, BY)
    wide = pl.ds(Y0, COLS)

    def coefficients(field, value_of):
        row = value_of(0)
        for i in range(ROWS):
            ahead = value_of(i + 1) if i + 1 < ROWS else row
            if i + 1 < ROWS:
                cx[field, i] = (row + ahead) * (0.5 * row_in(i) * row_in(i + 1))
            side = (row + pltpu.roll(row, COLS - 1, 0)) * col_face
            cy[field, i, wide, :] = side
            layer = jnp.where(top_lane, 0.0, 0.5 * (row + up(row)))
            czu[field, i] = layer
            under = down(layer)
            czd[field, i] = under
            if 0 < i < ROWS - 1:
                tile = first[i // BX, 3 * BX, :, :]
                shift = NZ - 1 - i % BX
                top = jnp.where(top_lane, pltpu.roll(tile, shift, 1), 0.0)
                diag = 1.0 + cx[field, i] + cx[field, i - 1] + side + pltpu.roll(side, 1, 0)
                diag = diag + layer + under + top * row
                inv[field, i] = (col_in * row_in(i)) / diag
            row = ahead

    def sweep(field, cur, nxt, lo, hi, right, y_at=0, y_size=COLS):
        here, span = pl.ds(Y0 + y_at, y_size), pl.ds(y_at, y_size)
        ahead, behind = pl.ds(Y0 + y_at + 1, y_size), pl.ds(Y0 + y_at - 1, y_size)
        west, mid = cur[lo - 1, here, :], cur[lo, here, :]
        face_west = cx[field, lo - 1, span, :]
        for i in range(lo, hi):
            east = cur[i + 1, here, :]
            face_east = cx[field, i, span, :]
            total = face_east * east + face_west * west
            total = total + cy[field, i, here, :] * cur[i, ahead, :]
            total = total + cy[field, i, behind, :] * cur[i, behind, :]
            total = total + czu[field, i, span, :] * up(mid) + czd[field, i, span, :] * down(mid)
            if right is not None:
                total = total + right[i, span, :]
            nxt[i, here, :] = total * inv[field, i, span, :]
            west, mid, face_west = mid, east, face_east

    def relax(field, even, odd, base, right):
        def body(t, carry):
            sweep(field, even.at[t], odd.at[t], 1, ROWS - 1, right)
            sweep(field, odd.at[t], even.at[t + 1], 2, ROWS - 2, right)
            return carry

        lax.fori_loop(base, base + 2, body, 0)
        sweep(field, even.at[base + 2], odd.at[base + 2], 5, ROWS - 5, right)
        sweep(field, odd.at[base + 2], even.at[base + 3], 6, ROWS - 6, right)
        sweep(field, even.at[base + 3], odd.at[base + 3], 7, ROWS - 7, right)
        sweep(field, odd.at[base + 3], even.at[base + 4], OX, OX + BX, right, HALO, BY)

    def top_of(r):
        tile = first[1, 3 * BX, own, :]
        return jnp.where(lane[:BY] == NZ - 1, pltpu.roll(tile, NZ - 1 - r, 1), 0.0)

    arrive(got_first)
    coefficients(HEAD, lambda i: first[i // BX, i % BX, :, :])
    for i in range(ROWS):
        start = first[i // BX, BX + i % BX, :, :]
        xe_head[0, i, wide, :] = start
        rhs[i] = start + first[i // BX, 2 * BX + i % BX, :, :]
    relax(HEAD, xe_head, xo_head, 0, rhs)
    got_head1 = exchange_field(2, xe_head, 4)
    started += got_head1

    arrive(got_second)
    coefficients(SOLUTE, lambda i: second[i // BX, i % BX, :, :])
    for i in range(ROWS):
        xe_solute[0, i, wide, :] = second[i // BX, BX + i % BX, :, :]
    for r in range(BX):
        lam_even[0, 0, OX + r, own_y, :] = solute_weight_in[r] * inv[SOLUTE, OX + r, own, :]
    got_lam_s2 = exchange_field(3, lam_even, 0, 0)
    started += got_lam_s2

    arrive(got_head1)
    for i in range(ROWS):
        rhs[i] = xe_head[4, i, wide, :] + first[i // BX, 2 * BX + i % BX, :, :]
    relax(HEAD, xe_head, xo_head, 4, rhs)
    got_head2 = exchange_field(4, xe_head, 8)
    started += got_head2

    for i in range(ROWS):
        rhs[i] = xe_solute[0, i, wide, :] + coupling_rate * xe_head[4, i, wide, :]
    relax(SOLUTE, xe_solute, xo_solute, 0, rhs)
    got_solute1 = exchange_field(5, xe_solute, 4)
    started += got_solute1

    arrive(got_head2)
    arrive(got_solute1)
    for i in range(ROWS):
        rhs[i] = xe_solute[4, i, wide, :] + coupling_rate * xe_head[8, i, wide, :]
    relax(SOLUTE, xe_solute, xo_solute, 4, rhs)
    got_solute2 = exchange_field(6, xe_solute, 8, dirs=DIRS[:4])
    started += got_solute2

    def retrace(field, which):
        relax(field, lam_even.at[which], lam_odd.at[which], 0, None)

    def right_bar(which, r):
        total = lam_even[which, 0, OX + r, own_y, :] + lam_odd[which, 0, OX + r, own_y, :]
        for k in range(1, 4):
            total = total + lam_even[which, k, OX + r, own_y, :]
            total = total + lam_odd[which, k, OX + r, own_y, :]
        return total

    arrive(got_lam_s2)
    retrace(SOLUTE, 0)
    for r in range(BX):
        bar = right_bar(0, r)
        lam_even[1, 0, OX + r, own_y, :] = (head_weight_in[r] + coupling_rate * bar) * inv[
            HEAD, OX + r, own, :
        ]
        lam_even[2, 0, OX + r, own_y, :] = (
            lam_even[0, 4, OX + r, own_y, :] + bar * inv[SOLUTE, OX + r, own, :]
        )
    got_lam_mid = exchange_field(7, lam_even, pl.ds(1, 2), 0)
    started += got_lam_mid

    acc_side[...] = jnp.zeros_like(acc_side)
    acc_layer[...] = jnp.zeros_like(acc_layer)
    acc_drop[...] = jnp.zeros_like(acc_drop)
    north_in = jnp.where(col[own] + 1 < GY * BY, 1.0, 0.0)
    south_in = jnp.where(col[own] > 0, 1.0, 0.0)
    east_in, west_in = row_in(OX + BX), row_in(OX - 1)

    def around(ref, lead, r):
        east, west = ref[(*lead, r + 1, own_y)], ref[(*lead, r - 1, own_y)]
        if r == OX + BX - 1:
            east = east * east_in
        if r == OX:
            west = west * west_in
        north = ref[(*lead, r, pl.ds(OY + 1, BY))] * north_in
        south = ref[(*lead, r, pl.ds(OY - 1, BY))] * south_in
        return east + west + north + south

    def gather(field, even, odd, base, which):
        def body(t, carry):
            steps = (
                ((lam_odd, (which, 3 - t)), (odd, (base + t,)), (even, (base + t,))),
                ((lam_even, (which, 3 - t)), (even, (base + t + 1,)), (odd, (base + t,))),
            )
            for r in range(OX, OX + BX):
                side = acc_side[field, r - OX]
                layer = acc_layer[field, r - OX]
                for (lam, at), _, (old, old_at) in steps:
                    lam_here = lam[(*at, r, own_y)]
                    old_here = old[(*old_at, r, own_y)]
                    side = side + lam_here * around(old, old_at, r)
                    side = side + old_here * around(lam, at, r)
                    layer = layer + lam_here * up(old_here) + old_here * up(lam_here)
                acc_side[field, r - OX] = side
                acc_layer[field, r - OX] = layer
            for r in range(OX - 1, OX + BX + 1):
                drop = acc_drop[field, r - OX + 1, wide, :]
                for (lam, at), (new, new_at), _ in steps:
                    drop = drop + lam[(*at, r, wide)] * new[(*new_at, r, wide)]
                acc_drop[field, r - OX + 1, wide, :] = drop
            return carry

        lax.fori_loop(0, 4, body, 0)

    arrive(got_solute2)
    gather(SOLUTE, xe_solute, xo_solute, 4, 0)
    for r in range(BX):
        head_out[r] = xe_head[8, OX + r, own_y, :]
        solute_out[r] = xe_solute[8, OX + r, own_y, :]

    arrive(got_lam_mid)
    retrace(HEAD, 1)
    retrace(SOLUTE, 2)
    for r in range(BX):
        bar = right_bar(1, r) + coupling_rate * right_bar(2, r)
        lam_even[3, 0, OX + r, own_y, :] = (
            lam_even[1, 4, OX + r, own_y, :] + bar * inv[HEAD, OX + r, own, :]
        )
    got_lam_h1 = exchange_field(8, lam_even, 3, 0)
    started += got_lam_h1
    gather(HEAD, xe_head, xo_head, 4, 1)
    gather(SOLUTE, xe_solute, xo_solute, 0, 2)

    arrive(got_lam_h1)
    retrace(HEAD, 3)
    gather(HEAD, xe_head, xo_head, 0, 3)

    own_lane = lane[:BY]
    inner_top = own_lane < NZ - 1
    inner_low = own_lane > 0

    def sensitivity(field, r):
        layer = jnp.where(inner_top, acc_layer[field, r], 0.0)
        drop = acc_drop[field, r + 1, own_y, :]
        east, west = acc_drop[field, r + 2, own_y, :], acc_drop[field, r, own_y, :]
        count = north_in + south_in
        if r == BX - 1:
            east = east * east_in
        if r == 0:
            west = west * west_in
        count = count + (east_in if r == BX - 1 else 1.0) + (west_in if r == 0 else 1.0)
        count = count + jnp.where(inner_top, 1.0, 0.0) + jnp.where(inner_low, 1.0, 0.0)
        total = acc_side[field, r] + layer + down(layer) - count * drop - east - west
        total = total - acc_drop[field, r + 1, pl.ds(OY + 1, BY), :] * north_in
        total = total - acc_drop[field, r + 1, pl.ds(OY - 1, BY), :] * south_in
        total = total - jnp.where(inner_top, up(drop), 0.0) - jnp.where(inner_low, down(drop), 0.0)
        return 0.5 * total - top_of(r) * drop

    sums = [jnp.zeros((BY, NZ), jnp.float32) for _ in range(MATS)]
    for r in range(BX):
        conductivity = first[1, r, own, :]
        spread_bar = sensitivity(SOLUTE, r)
        total_bar = sensitivity(HEAD, r) + disp_in[r] * spread_bar
        scaled = total_bar * conductivity
        grad_cond_out[r] = scaled
        grad_disp_out[r] = spread_bar * conductivity
        material = material_in[r]
        for m in range(MATS):
            sums[m] = sums[m] + jnp.where(material == m, scaled, 0.0)
    mat_row = lax.broadcasted_iota(jnp.int32, (MATS, NZ), 0)
    partial = jnp.zeros((MATS, NZ), jnp.float32)
    for m in range(MATS):
        partial = jnp.where(mat_row == m, jnp.sum(sums[m], axis=0, keepdims=True), partial)

    def reduce(part, at, device_of, sends, recvs, value):
        part[at] = value
        copies = []
        for t in range(1, 16):
            copies.append(
                pltpu.make_async_remote_copy(
                    src_ref=part.at[at],
                    dst_ref=part.at[at],
                    send_sem=sends.at[t],
                    recv_sem=recvs.at[t],
                    device_id=device_of(t),
                    device_id_type=MESH,
                )
            )
            copies[-1].start()
        for t in range(1, 16):
            slot = lax.rem(at - t + 16, 16)
            pltpu.make_async_remote_copy(
                src_ref=part.at[slot],
                dst_ref=part.at[slot],
                send_sem=sends.at[t],
                recv_sem=recvs.at[t],
                device_id=device_of(t),
                device_id_type=MESH,
            ).wait_recv()
        total = part[0]
        for k in range(1, 16):
            total = total + part[k]
        return copies, total

    copies, partial = reduce(part_a, a_at, a_device, send_a, recv_a, partial)
    started += copies
    copies, partial = reduce(part_b, b_at, b_device, send_b, recv_b, partial)
    started += copies
    base = jnp.ones((MATS, NZ), jnp.float32)
    for m in range(MATS):
        base = jnp.where(mat_row == m, table_in[m], base)
    summed = jnp.sum(partial, axis=1, keepdims=True)
    grad_table_out[...] = jnp.broadcast_to(summed, (MATS, NZ)) / base
    for copy in started:
        copy.wait_send()


def local(*arrays):
    block = jax.ShapeDtypeStruct((BX, BY, NZ), jnp.float32)
    vmem = pl.BlockSpec(memory_space=pltpu.VMEM)
    smem = pl.BlockSpec(memory_space=pltpu.SMEM)
    f32 = jnp.float32
    outs = pl.pallas_call(
        kernel,
        out_shape=(block, block, block, block, jax.ShapeDtypeStruct((MATS, NZ), f32)),
        in_specs=[smem if k == 6 else vmem for k in range(10)],
        out_specs=(vmem,) * 5,
        scratch_shapes=[
            pltpu.VMEM((3, 3 * BX + 1, COLS, NZ), f32),
            pltpu.VMEM((3, 2 * BX, COLS, NZ), f32),
            pltpu.VMEM((2, ROWS, COLS, NZ), f32),
            pltpu.VMEM((2, ROWS, PAD, NZ), f32),
            pltpu.VMEM((2, ROWS, COLS, NZ), f32),
            pltpu.VMEM((2, ROWS, COLS, NZ), f32),
            pltpu.VMEM((2, ROWS, COLS, NZ), f32),
            pltpu.VMEM((ROWS, COLS, NZ), f32),
            pltpu.VMEM((9, ROWS, PAD, NZ), f32),
            pltpu.VMEM((8, ROWS, PAD, NZ), f32),
            pltpu.VMEM((9, ROWS, PAD, NZ), f32),
            pltpu.VMEM((8, ROWS, PAD, NZ), f32),
            pltpu.VMEM((4, 5, ROWS, PAD, NZ), f32),
            pltpu.VMEM((4, 4, ROWS, PAD, NZ), f32),
            pltpu.VMEM((2, BX, BY, NZ), f32),
            pltpu.VMEM((2, BX, BY, NZ), f32),
            pltpu.VMEM((2, BX + 2, PAD, NZ), f32),
            pltpu.VMEM((16, MATS, NZ), f32),
            pltpu.VMEM((16, MATS, NZ), f32),
            pltpu.SemaphoreType.DMA((9, 8)),
            pltpu.SemaphoreType.DMA((9, 8)),
            pltpu.SemaphoreType.DMA((16,)),
            pltpu.SemaphoreType.DMA((16,)),
            pltpu.SemaphoreType.DMA((16,)),
            pltpu.SemaphoreType.DMA((16,)),
        ],
        compiler_params=pltpu.CompilerParams(
            collective_id=0, has_side_effects=True, vmem_limit_bytes=58 << 20
        ),
        name="window",
    )(*arrays)
    return (*outs[:4], outs[4][:, 0])


def solution(mesh):
    block = P("gx", "gy", None)
    return jax.shard_map(
        local,
        mesh=mesh,
        in_specs=(block, block, block, block, block, block, P(), P("gx", "gy"), block, block),
        out_specs=(block, block, block, block, P()),
        check_vma=False,
    )
```

```python
import jax
import jax.numpy as jnp
from jax import lax
from jax.experimental import pallas as pl
from jax.experimental.pallas import tpu as pltpu
from jax.sharding import PartitionSpec as P

SWEEPS = 8
MATS = 8
coupling_rate = 0.5

BX, BY, NZ, HALO = 8, 16, 128, 8
GX, GY = 32, 8
ROWS = BX + 2 * HALO
COLS = BY + 2 * HALO
PAD = COLS + 16
Y0, Y1 = 8, 8 + COLS
OX, OY = HALO, 8 + HALO
MESH = pl.DeviceIdType.MESH
DIRS = ((1, 0), (-1, 0), (0, 1), (0, -1), (1, 1), (1, -1), (-1, 1), (-1, -1))
FAR = ((2, 0), (-2, 0))
FACES, CORNERS = DIRS[:4], DIRS[4:]
TILES = 50
HEAD, SOLUTE = 0, 1


def place(lx, ly):
    return (lax.rem(lx + GX, GX), lax.rem(ly + GY, GY))


def x_part(dx):
    return {0: slice(OX, OX + BX), 1: slice(0, HALO), -1: slice(OX + BX, ROWS)}[dx]


def y_from(dy):
    return {0: (0, BY), 1: (BY - HALO, HALO), -1: (0, HALO)}[dy]


def y_into(dy):
    return {0: (HALO, BY), 1: (0, HALO), -1: (HALO + BY, HALO)}[dy]


CORNER_ROWS = {
    8: ((1, 7, 7), (2, 6, 6), (3, 5, 5), (4, None, 4)),
    9: ((1, None, 8), (2, 8, 7), (3, 7, 6), (4, 6, 5), (5, None, 4)),
}


def up(cells):
    return pltpu.roll(cells, NZ - 1, 1)


def down(cells):
    return pltpu.roll(cells, 1, 1)


def kernel(
    head_in,
    solute_in,
    source_in,
    log_in,
    disp_in,
    material_in,
    table_in,
    boundary_in,
    head_weight_in,
    solute_weight_in,
    fields_out,
    grad_table_out,
    first,
    second,
    far_x,
    far_y,
    corner_out,
    corner_in,
    cx,
    cy,
    czu,
    czd,
    inv,
    rhs,
    xe_head,
    xo_head,
    xe_solute,
    xo_solute,
    lam_even,
    lam_odd,
    acc_side,
    acc_layer,
    acc_drop,
    part_a,
    part_b,
    send_sem,
    recv_sem,
    send_far,
    recv_far,
    send_a,
    recv_a,
    send_b,
    recv_b,
):
    gx, gy = lax.axis_index("gx"), lax.axis_index("gy")
    lx, ly = gx, gy
    neighbours = {d: place(lx + d[0], ly + d[1]) for d in (*DIRS, *FAR)}
    z_at, hi_at, core_at = gx // 4, lax.rem(gx // 2, 2), lax.rem(gx, 2)
    a_at = hi_at * 8 + gy
    b_at = z_at * 2 + core_at

    def a_device(t):
        to = lax.rem(a_at + t, 16)
        return (z_at * 4 + (to // 8) * 2 + core_at, lax.rem(to, 8))

    def b_device(t):
        to = lax.rem(b_at + t, 16)
        return ((to // 2) * 4 + hi_at * 2 + lax.rem(to, 2), gy)

    barrier = pltpu.get_barrier_semaphore()
    for d in (*DIRS, *FAR):
        pl.semaphore_signal(barrier, inc=1, device_id=neighbours[d], device_id_type=MESH)
    for t in range(1, 16):
        pl.semaphore_signal(barrier, inc=1, device_id=a_device(t), device_id_type=MESH)
        pl.semaphore_signal(barrier, inc=1, device_id=b_device(t), device_id_type=MESH)

    lane = lax.broadcasted_iota(jnp.int32, (COLS, NZ), 1)
    col = lax.broadcasted_iota(jnp.int32, (COLS, NZ), 0) + (ly * BY - HALO)
    col_in = jnp.where((col >= 0) & (col < GY * BY), 1.0, 0.0)
    col_face = jnp.where((col >= 0) & (col + 1 < GY * BY), 0.5, 0.0)
    top_lane = lane == NZ - 1

    def row_in(i):
        at = lx * BX + (i - HALO)
        return jnp.where((at >= 0) & (at < GX * BX), 1.0, 0.0)

    own = slice(HALO, HALO + BY)
    own_y = pl.ds(OY, BY)
    wide = pl.ds(Y0, COLS)
    for r in range(BX):
        material = material_in[r]
        base = jnp.zeros((BY, NZ), jnp.float32)
        for m in range(MATS):
            base = jnp.where(material == m, table_in[m], base)
        conductivity = base * jnp.exp(log_in[r])
        first[1, r, own, :] = conductivity
        first[1, BX + r, own, :] = head_in[r]
        first[1, 2 * BX + r, own, :] = source_in[r]
        second[1, r, own, :] = disp_in[r] * conductivity
        second[1, BX + r, own, :] = solute_weight_in[r]
        xe_solute[0, OX + r, own_y, :] = solute_in[r]
    kind = boundary_in[...]
    factor = jnp.where(kind == 1, 1.0, jnp.where(kind == 2, 4.0, 0.0)).astype(jnp.float32)
    diagonal_at = lax.broadcasted_iota(jnp.int32, (BY, BY), 0) == lax.broadcasted_iota(
        jnp.int32, (BY, BY), 1
    )
    tops = jnp.zeros((BY, NZ), jnp.float32)
    for r in range(BX):
        spread = jnp.broadcast_to(factor[r : r + 1, :], (BY, BY))
        column = jnp.sum(jnp.where(diagonal_at, spread, 0.0), axis=1, keepdims=True)
        tops = jnp.where(lane[:BY] == r, column, tops)
    first[1, 3 * BX, own, :] = tops

    pl.semaphore_wait(barrier, len(DIRS) + len(FAR) + 30)

    near = lax.broadcasted_iota(jnp.int32, (HALO, NZ), 0)

    def launch(event, d, source, target):
        k = DIRS.index(d)
        copy = pltpu.make_async_remote_copy(
            src_ref=source,
            dst_ref=target,
            send_sem=send_sem.at[event, k],
            recv_sem=recv_sem.at[event, k],
            device_id=neighbours[d],
            device_id_type=MESH,
        )
        copy.start()
        return copy

    def exchange(event, source_of, target_of, base, fields, extra=None):
        copies = [launch(event, d, source_of(d), target_of(d)) for d in FACES]
        for k, (dx, dy) in enumerate(CORNERS):
            at = base
            for radius, read, _ in fields:
                for d, partner, cells in CORNER_ROWS[radius]:
                    tile = read(d, dx, dy)
                    if partner is not None:
                        other = read(partner, dx, dy)
                        if dy > 0:
                            tile = jnp.where(near >= HALO - cells, tile, pltpu.roll(other, HALO - cells, 0))
                        else:
                            tile = jnp.where(near < cells, tile, pltpu.roll(other, cells, 0))
                    corner_out[k, at] = tile
                    at += 1
            if extra is not None:
                corner_out[k, at] = extra[0](dx, dy)
                at += 1
            part = pl.ds(base, at - base)
            copies.append(launch(event, (dx, dy), corner_out.at[k, part], corner_in.at[k, part]))

        def lay():
            for k, (dx, dy) in enumerate(CORNERS):
                at = base
                for radius, _, write in fields:
                    for d, partner, cells in CORNER_ROWS[radius]:
                        tile = corner_in[k, at]
                        write(d, dx, dy, tile)
                        if partner is not None:
                            back = cells if dy > 0 else HALO - cells
                            write(partner, dx, dy, pltpu.roll(tile, back, 0))
                        at += 1
                if extra is not None:
                    extra[1](dx, dy, corner_in[k, at])

        started.extend(copies)
        return copies, lay

    def exchange_pack(event, pack, base, radii, extra=None):
        def source_of(d):
            first_col, size = y_from(d[1])
            return pack.at[1, :, pl.ds(HALO + first_col, size), :]

        def target_of(d):
            first_col, size = y_into(d[1])
            return pack.at[1 - d[0], :, pl.ds(first_col, size), :]

        def field(f, radius):
            def row(d, dx):
                return f * BX + (BX - d if dx > 0 else d - 1)

            def read(d, dx, dy):
                return pack[1, row(d, dx), pl.ds(HALO + y_from(dy)[0], HALO), :]

            def write(d, dx, dy, tile):
                pack[1 - dx, row(d, dx), pl.ds(y_into(dy)[0], HALO), :] = tile

            return radius, read, write

        fields = [field(f, radius) for f, radius in enumerate(radii)]
        if extra is not None:
            at = extra
            extra = (
                lambda dx, dy: pack[1, at, pl.ds(HALO + y_from(dy)[0], HALO), :],
                lambda dx, dy, tile: pack.__setitem__(
                    (1 - dx, at, pl.ds(y_into(dy)[0], HALO), slice(None)), tile
                ),
            )
        return exchange(event, source_of, target_of, base, fields, extra)

    def exchange_field(event, ref, base, *leads, faces=None):
        lead_all = faces or leads[0]

        def source_of(d):
            first_col, size = y_from(d[1])
            return ref.at[(*lead_all, pl.ds(OX, BX), pl.ds(OY + first_col, size), slice(None))]

        def target_of(d):
            first_col, size = y_into(d[1])
            part = x_part(d[0])
            rows = pl.ds(part.start, part.stop - part.start)
            return ref.at[(*lead_all, rows, pl.ds(Y0 + first_col, size), slice(None))]

        def field(lead):
            def read(d, dx, dy):
                row = OX + BX - d if dx > 0 else OX + d - 1
                return ref[(*lead, row, pl.ds(OY + y_from(dy)[0], HALO))]

            def write(d, dx, dy, tile):
                row = OX - d if dx > 0 else OX + BX - 1 + d
                ref[(*lead, row, pl.ds(Y0 + y_into(dy)[0], HALO))] = tile

            return HALO, read, write

        if base is None:
            copies = [launch(event, d, source_of(d), target_of(d)) for d in FACES]
            started.extend(copies)
            return copies, None
        return exchange(event, source_of, target_of, base, [field(lead) for lead in leads])

    def arrive(got):
        copies, lay = got
        for copy in copies:
            copy.wait_recv()
        if lay is not None:
            lay()

    def send_to(d, source, target, k):
        copy = pltpu.make_async_remote_copy(
            src_ref=source,
            dst_ref=target,
            send_sem=send_far.at[k],
            recv_sem=recv_far.at[k],
            device_id=neighbours[d],
            device_id_type=MESH,
        )
        copy.start()
        return copy

    started = []
    got_first = exchange_pack(0, first, 0, (8, 8, 8), 3 * BX)
    got_second = exchange_pack(1, second, 13, (9, 8))
    rows = pl.ds(0, BX)
    got_far = [
        send_to((2, 0), second.at[1, BX - 1, pl.ds(HALO, BY), :], far_x.at[0], 0),
        send_to((-2, 0), second.at[1, 0, pl.ds(HALO, BY), :], far_x.at[1], 1),
        send_to((0, 1), second.at[1, rows, pl.ds(HALO, HALO), :], far_y.at[0], 2),
        send_to((0, -1), second.at[1, rows, pl.ds(BY, HALO), :], far_y.at[1], 3),
    ]
    started += got_far
    got_start = exchange_field(2, xe_solute, 22, (0,))

    at_low, at_high = col == ly * BY - HALO, col == ly * BY + BY + HALO - 1
    low_face = jnp.where(at_low & (col > 0) & (col < GY * BY), 0.5, 0.0)

    def coefficients(field, value_of, beyond):
        row = value_of(0)
        face_before = None
        if beyond:
            face_before = (value_of(-1) + row) * (0.5 * row_in(-1) * row_in(0))
        for i in range(ROWS):
            face = None
            if beyond or i + 1 < ROWS:
                ahead = value_of(i + 1)
                face = (row + ahead) * (0.5 * row_in(i) * row_in(i + 1))
                if i + 1 < ROWS:
                    cx[field, i] = face
            north = pltpu.roll(row, COLS - 1, 0)
            far = beyond and OX <= i < OX + BX
            if far:
                north = jnp.where(at_high, far_y[1, i - OX, 0:1, :], north)
            side = (row + north) * col_face
            cy[field, i, wide, :] = side
            layer = jnp.where(top_lane, 0.0, 0.5 * (row + up(row)))
            czu[field, i] = layer
            under = down(layer)
            czd[field, i] = under
            if face is not None and face_before is not None:
                south = pltpu.roll(side, 1, 0)
                if far:
                    low = (row + far_y[0, i - OX, HALO - 1 : HALO, :]) * low_face
                    south = jnp.where(at_low, low, south)
                tile = first[i // BX, 3 * BX, :, :]
                top = jnp.where(top_lane, pltpu.roll(tile, NZ - 1 - i % BX, 1), 0.0)
                diag = 1.0 + face + face_before + side + south + layer + under + top * row
                inv[field, i] = (col_in * row_in(i)) / diag
            if face is not None:
                row, face_before = ahead, face

    def sweep(field, cur, nxt, lo, hi, right, y_at=0, y_size=COLS):
        here, span = pl.ds(Y0 + y_at, y_size), pl.ds(y_at, y_size)
        ahead, behind = pl.ds(Y0 + y_at + 1, y_size), pl.ds(Y0 + y_at - 1, y_size)
        west, mid = cur[lo - 1, here, :], cur[lo, here, :]
        face_west = cx[field, lo - 1, span, :]
        for i in range(lo, hi):
            east = cur[i + 1, here, :]
            face_east = cx[field, i, span, :]
            total = face_east * east + face_west * west
            total = total + cy[field, i, here, :] * cur[i, ahead, :]
            total = total + cy[field, i, behind, :] * cur[i, behind, :]
            total = total + czu[field, i, span, :] * up(mid) + czd[field, i, span, :] * down(mid)
            if right is not None:
                total = total + right[i, span, :]
            nxt[i, here, :] = total * inv[field, i, span, :]
            west, mid, face_west = mid, east, face_east

    def relax(field, even, odd, base, right):
        def body(t, carry):
            sweep(field, even.at[t], odd.at[t], 1, ROWS - 1, right)
            sweep(field, odd.at[t], even.at[t + 1], 2, ROWS - 2, right)
            return carry

        lax.fori_loop(base, base + 2, body, 0)
        sweep(field, even.at[base + 2], odd.at[base + 2], 5, ROWS - 5, right)
        sweep(field, odd.at[base + 2], even.at[base + 3], 6, ROWS - 6, right)
        sweep(field, even.at[base + 3], odd.at[base + 3], 7, ROWS - 7, right)
        sweep(field, odd.at[base + 3], even.at[base + 4], OX, OX + BX, right, HALO, BY)

    def top_of(r):
        tile = first[1, 3 * BX, own, :]
        return jnp.where(lane[:BY] == NZ - 1, pltpu.roll(tile, NZ - 1 - r, 1), 0.0)

    def retrace(field, which):
        relax(field, lam_even.at[which], lam_odd.at[which], 0, None)

    def right_bar(which, r):
        total = lam_even[which, 0, OX + r, own_y, :] + lam_odd[which, 0, OX + r, own_y, :]
        for k in range(1, 4):
            total = total + lam_even[which, k, OX + r, own_y, :]
            total = total + lam_odd[which, k, OX + r, own_y, :]
        return total

    acc_side[...] = jnp.zeros_like(acc_side)
    acc_layer[...] = jnp.zeros_like(acc_layer)
    acc_drop[...] = jnp.zeros_like(acc_drop)
    north_in = jnp.where(col[own] + 1 < GY * BY, 1.0, 0.0)
    south_in = jnp.where(col[own] > 0, 1.0, 0.0)
    east_in, west_in = row_in(OX + BX), row_in(OX - 1)

    def around(ref, lead, r):
        east, west = ref[(*lead, r + 1, own_y)], ref[(*lead, r - 1, own_y)]
        if r == OX + BX - 1:
            east = east * east_in
        if r == OX:
            west = west * west_in
        north = ref[(*lead, r, pl.ds(OY + 1, BY))] * north_in
        south = ref[(*lead, r, pl.ds(OY - 1, BY))] * south_in
        return east + west + north + south

    def gather(field, even, odd, base, which):
        def body(t, carry):
            steps = (
                ((lam_odd, (which, 3 - t)), (odd, (base + t,)), (even, (base + t,))),
                ((lam_even, (which, 3 - t)), (even, (base + t + 1,)), (odd, (base + t,))),
            )
            for r in range(OX, OX + BX):
                side = acc_side[field, r - OX]
                layer = acc_layer[field, r - OX]
                for (lam, at), _, (old, old_at) in steps:
                    lam_here = lam[(*at, r, own_y)]
                    old_here = old[(*old_at, r, own_y)]
                    side = side + lam_here * around(old, old_at, r)
                    side = side + old_here * around(lam, at, r)
                    layer = layer + lam_here * up(old_here) + old_here * up(lam_here)
                acc_side[field, r - OX] = side
                acc_layer[field, r - OX] = layer
            for r in range(OX - 1, OX + BX + 1):
                drop = acc_drop[field, r - OX + 1, wide, :]
                for (lam, at), (new, new_at), _ in steps:
                    drop = drop + lam[(*at, r, wide)] * new[(*new_at, r, wide)]
                acc_drop[field, r - OX + 1, wide, :] = drop
            return carry

        lax.fori_loop(0, 4, body, 0)

    arrive(got_first)
    coefficients(HEAD, lambda i: first[i // BX, i % BX, :, :], False)
    for i in range(ROWS):
        start = first[i // BX, BX + i % BX, :, :]
        xe_head[0, i, wide, :] = start
        rhs[i] = start + first[i // BX, 2 * BX + i % BX, :, :]
    relax(HEAD, xe_head, xo_head, 0, rhs)
    got_head1 = exchange_field(3, xe_head, 26, (4,))

    arrive(got_second)
    arrive((got_far, None))

    def spreading(i):
        if 0 <= i < ROWS:
            return second[i // BX, i % BX, :, :]
        beyond = far_x[0 if i < 0 else 1]
        return jnp.concatenate([beyond[:HALO], beyond, beyond[:HALO]], axis=0)

    coefficients(SOLUTE, spreading, True)
    for i in range(ROWS):
        lam_even[0, 0, i, wide, :] = second[i // BX, BX + i % BX, :, :] * inv[SOLUTE, i]
    retrace(SOLUTE, 0)
    for r in range(BX):
        bar = right_bar(0, r)
        lam_even[1, 0, OX + r, own_y, :] = (head_weight_in[r] + coupling_rate * bar) * inv[
            HEAD, OX + r, own, :
        ]
        lam_even[2, 0, OX + r, own_y, :] = (
            lam_even[0, 4, OX + r, own_y, :] + bar * inv[SOLUTE, OX + r, own, :]
        )
    got_lam_mid = exchange_field(4, lam_even, 30, (1, 0), (2, 0), faces=(pl.ds(1, 2), 0))

    arrive(got_head1)
    for i in range(ROWS):
        rhs[i] = xe_head[4, i, wide, :] + first[i // BX, 2 * BX + i % BX, :, :]
    relax(HEAD, xe_head, xo_head, 4, rhs)
    got_head2 = exchange_field(5, xe_head, 38, (8,))
    arrive(got_start)
    for i in range(ROWS):
        rhs[i] = xe_solute[0, i, wide, :] + coupling_rate * xe_head[4, i, wide, :]
    relax(SOLUTE, xe_solute, xo_solute, 0, rhs)
    got_solute1 = exchange_field(6, xe_solute, 42, (4,))
    arrive(got_lam_mid)
    retrace(HEAD, 1)
    retrace(SOLUTE, 2)
    for r in range(BX):
        bar = right_bar(1, r) + coupling_rate * right_bar(2, r)
        lam_even[3, 0, OX + r, own_y, :] = (
            lam_even[1, 4, OX + r, own_y, :] + bar * inv[HEAD, OX + r, own, :]
        )
    got_lam_h1 = exchange_field(7, lam_even, 46, (3, 0))

    arrive(got_head2)
    arrive(got_solute1)
    for i in range(ROWS):
        rhs[i] = xe_solute[4, i, wide, :] + coupling_rate * xe_head[8, i, wide, :]
    relax(SOLUTE, xe_solute, xo_solute, 4, rhs)
    got_solute2 = exchange_field(8, xe_solute, None, (8,))
    gather(HEAD, xe_head, xo_head, 4, 1)
    gather(SOLUTE, xe_solute, xo_solute, 0, 2)
    arrive(got_lam_h1)
    retrace(HEAD, 3)
    gather(HEAD, xe_head, xo_head, 0, 3)
    for r in range(BX):
        fields_out[0, r] = xe_head[8, OX + r, own_y, :]
        fields_out[1, r] = xe_solute[8, OX + r, own_y, :]
    arrive(got_solute2)
    gather(SOLUTE, xe_solute, xo_solute, 4, 0)

    own_lane = lane[:BY]
    inner_top = own_lane < NZ - 1
    inner_low = own_lane > 0

    def sensitivity(field, r):
        layer = jnp.where(inner_top, acc_layer[field, r], 0.0)
        drop = acc_drop[field, r + 1, own_y, :]
        east, west = acc_drop[field, r + 2, own_y, :], acc_drop[field, r, own_y, :]
        count = north_in + south_in
        if r == BX - 1:
            east = east * east_in
        if r == 0:
            west = west * west_in
        count = count + (east_in if r == BX - 1 else 1.0) + (west_in if r == 0 else 1.0)
        count = count + jnp.where(inner_top, 1.0, 0.0) + jnp.where(inner_low, 1.0, 0.0)
        total = acc_side[field, r] + layer + down(layer) - count * drop - east - west
        total = total - acc_drop[field, r + 1, pl.ds(OY + 1, BY), :] * north_in
        total = total - acc_drop[field, r + 1, pl.ds(OY - 1, BY), :] * south_in
        total = total - jnp.where(inner_top, up(drop), 0.0) - jnp.where(inner_low, down(drop), 0.0)
        return 0.5 * total - top_of(r) * drop

    sums = [jnp.zeros((BY, NZ), jnp.float32) for _ in range(MATS)]
    for r in range(BX):
        conductivity = first[1, r, own, :]
        spread_bar = sensitivity(SOLUTE, r)
        total_bar = sensitivity(HEAD, r) + disp_in[r] * spread_bar
        scaled = total_bar * conductivity
        fields_out[2, r] = scaled
        fields_out[3, r] = spread_bar * conductivity
        material = material_in[r]
        for m in range(MATS):
            sums[m] = sums[m] + jnp.where(material == m, scaled, 0.0)
    mat_row = lax.broadcasted_iota(jnp.int32, (MATS, NZ), 0)
    partial = jnp.zeros((MATS, NZ), jnp.float32)
    for m in range(MATS):
        partial = jnp.where(mat_row == m, jnp.sum(sums[m], axis=0, keepdims=True), partial)

    def reduce(part, at, device_of, sends, recvs, value):
        part[at] = value
        copies = []
        for t in range(1, 16):
            copies.append(
                pltpu.make_async_remote_copy(
                    src_ref=part.at[at],
                    dst_ref=part.at[at],
                    send_sem=sends.at[t],
                    recv_sem=recvs.at[t],
                    device_id=device_of(t),
                    device_id_type=MESH,
                )
            )
            copies[-1].start()
        for t in range(1, 16):
            slot = lax.rem(at - t + 16, 16)
            pltpu.make_async_remote_copy(
                src_ref=part.at[slot],
                dst_ref=part.at[slot],
                send_sem=sends.at[t],
                recv_sem=recvs.at[t],
                device_id=device_of(t),
                device_id_type=MESH,
            ).wait_recv()
        total = part[0]
        for k in range(1, 16):
            total = total + part[k]
        return copies, total

    copies, partial = reduce(part_a, a_at, a_device, send_a, recv_a, partial)
    started += copies
    copies, partial = reduce(part_b, b_at, b_device, send_b, recv_b, partial)
    started += copies
    base = jnp.ones((MATS, NZ), jnp.float32)
    for m in range(MATS):
        base = jnp.where(mat_row == m, table_in[m], base)
    summed = jnp.sum(partial, axis=1, keepdims=True)
    grad_table_out[...] = jnp.broadcast_to(summed, (MATS, NZ)) / base
    for copy in started:
        copy.wait_send()


def hand_over(fields, table, head_out, solute_out, grad_cond_out, grad_disp_out, grad_table_out):
    for k, out in enumerate((head_out, solute_out, grad_cond_out, grad_disp_out)):
        out[...] = fields[k]
    for m in range(MATS):
        grad_table_out[m] = table[m, 0]


def local(*arrays):
    f32 = jnp.float32
    block = jax.ShapeDtypeStruct((BX, BY, NZ), f32)
    vmem = pl.BlockSpec(memory_space=pltpu.VMEM)
    smem = pl.BlockSpec(memory_space=pltpu.SMEM)
    fields, table = pl.pallas_call(
        kernel,
        out_shape=(
            jax.ShapeDtypeStruct((4, BX, BY, NZ), f32),
            jax.ShapeDtypeStruct((MATS, NZ), f32),
        ),
        in_specs=[smem if k == 6 else vmem for k in range(10)],
        out_specs=(vmem, vmem),
        scratch_shapes=[
            pltpu.VMEM((3, 3 * BX + 1, COLS, NZ), f32),
            pltpu.VMEM((3, 2 * BX, COLS, NZ), f32),
            pltpu.VMEM((2, BY, NZ), f32),
            pltpu.VMEM((2, BX, HALO, NZ), f32),
            pltpu.VMEM((4, TILES, HALO, NZ), f32),
            pltpu.VMEM((4, TILES, HALO, NZ), f32),
            pltpu.VMEM((2, ROWS, COLS, NZ), f32),
            pltpu.VMEM((2, ROWS, PAD, NZ), f32),
            pltpu.VMEM((2, ROWS, COLS, NZ), f32),
            pltpu.VMEM((2, ROWS, COLS, NZ), f32),
            pltpu.VMEM((2, ROWS, COLS, NZ), f32),
            pltpu.VMEM((ROWS, COLS, NZ), f32),
            pltpu.VMEM((9, ROWS, PAD, NZ), f32),
            pltpu.VMEM((8, ROWS, PAD, NZ), f32),
            pltpu.VMEM((9, ROWS, PAD, NZ), f32),
            pltpu.VMEM((8, ROWS, PAD, NZ), f32),
            pltpu.VMEM((4, 5, ROWS, PAD, NZ), f32),
            pltpu.VMEM((4, 4, ROWS, PAD, NZ), f32),
            pltpu.VMEM((2, BX, BY, NZ), f32),
            pltpu.VMEM((2, BX, BY, NZ), f32),
            pltpu.VMEM((2, BX + 2, PAD, NZ), f32),
            pltpu.VMEM((16, MATS, NZ), f32),
            pltpu.VMEM((16, MATS, NZ), f32),
            pltpu.SemaphoreType.DMA((9, 8)),
            pltpu.SemaphoreType.DMA((9, 8)),
            pltpu.SemaphoreType.DMA((4,)),
            pltpu.SemaphoreType.DMA((4,)),
            pltpu.SemaphoreType.DMA((16,)),
            pltpu.SemaphoreType.DMA((16,)),
            pltpu.SemaphoreType.DMA((16,)),
            pltpu.SemaphoreType.DMA((16,)),
        ],
        compiler_params=pltpu.CompilerParams(
            collective_id=0, has_side_effects=True, vmem_limit_bytes=58 << 20
        ),
        name="window",
    )(*arrays)
    return pl.pallas_call(
        hand_over,
        out_shape=(block, block, block, block, jax.ShapeDtypeStruct((MATS,), f32)),
        in_specs=[vmem, vmem],
        out_specs=(vmem,) * 4 + (smem,),
        name="hand_over",
    )(fields, table)


def solution(mesh):
    block = P("gx", "gy", None)
    return jax.shard_map(
        local,
        mesh=mesh,
        in_specs=(block, block, block, block, block, block, P(), P("gx", "gy"), block, block),
        out_specs=(block, block, block, block, P()),
        check_vma=False,
    )
```

```python
import jax
import jax.numpy as jnp
from jax import lax
from jax.experimental import pallas as pl
from jax.experimental.pallas import tpu as pltpu
from jax.sharding import PartitionSpec as P

SWEEPS = 8
MATS = 8
coupling_rate = 0.5

BX, BY, NZ, HALO = 8, 16, 128, 8
GX, GY = 32, 8
ROWS = BX + 2 * HALO
COLS = BY + 2 * HALO
PAD = COLS + 16
Y0, Y1 = 8, 8 + COLS
OX, OY = HALO, 8 + HALO
MESH = pl.DeviceIdType.MESH
DIRS = ((1, 0), (-1, 0), (0, 1), (0, -1), (1, 1), (1, -1), (-1, 1), (-1, -1))
FAR = ((2, 0), (-2, 0))
FACES, CORNERS = DIRS[:4], DIRS[4:]
TILES = 50
HEAD, SOLUTE = 0, 1


def host_of(bx, by):
    z, half = bx // 4, by // 4
    pair = lax.rem(lax.rem(bx // 2, 2) + z, 2)
    x = jnp.where(half == 0, pair, 3 - pair)
    y = jnp.where(half == 0, lax.rem(by, 4), 3 - lax.rem(by, 4))
    return (z * 4 + (x // 2) * 2 + lax.rem(bx, 2), lax.rem(x, 2) * 4 + y)


def block_of(gx, gy):
    z, x, y = gx // 4, lax.rem(gx // 2, 2) * 2 + gy // 4, lax.rem(gy, 4)
    half = x // 2
    pair = jnp.where(half == 0, x, 3 - x)
    high = lax.rem(pair + z, 2)
    return (z * 4 + high * 2 + lax.rem(gx, 2), half * 4 + jnp.where(half == 0, y, 3 - y))


def place(bx, by):
    return host_of(lax.rem(bx + GX, GX), lax.rem(by + GY, GY))


def x_part(dx):
    return {0: slice(OX, OX + BX), 1: slice(0, HALO), -1: slice(OX + BX, ROWS)}[dx]


def y_from(dy):
    return {0: (0, BY), 1: (BY - HALO, HALO), -1: (0, HALO)}[dy]


def y_into(dy):
    return {0: (HALO, BY), 1: (0, HALO), -1: (HALO + BY, HALO)}[dy]


CORNER_ROWS = {
    8: ((1, 7, 7), (2, 6, 6), (3, 5, 5), (4, None, 4)),
    9: ((1, None, 8), (2, 8, 7), (3, 7, 6), (4, 6, 5), (5, None, 4)),
}


def up(cells):
    return pltpu.roll(cells, NZ - 1, 1)


def down(cells):
    return pltpu.roll(cells, 1, 1)


def kernel(
    head_hbm,
    solute_hbm,
    source_hbm,
    log_hbm,
    disp_hbm,
    material_hbm,
    table_in,
    boundary_hbm,
    head_weight_hbm,
    solute_weight_hbm,
    fields_out,
    grad_table_out,
    log_in,
    material_in,
    boundary_in,
    head_weight_in,
    grads,
    material_home,
    disp_home,
    made,
    tops_home,
    load_sem,
    store_sem,
    store_send,
    move_send,
    move_recv,
    first,
    second,
    far_x,
    far_y,
    corner_out,
    corner_in,
    cx,
    cy,
    czu,
    inv,
    rhs,
    xe_head,
    xo_head,
    xe_solute,
    xo_solute,
    lam_even,
    lam_odd,
    acc_side,
    acc_layer,
    acc_drop,
    part_a,
    part_b,
    send_sem,
    recv_sem,
    send_far,
    recv_far,
    send_a,
    recv_a,
    send_b,
    recv_b,
):
    gx, gy = lax.axis_index("gx"), lax.axis_index("gy")
    lx, ly = block_of(gx, gy)
    host, home = host_of(gx, gy), (lx, ly)
    stays = (lx == gx) & (ly == gy)
    moves = jnp.logical_not(stays)
    neighbours = {d: place(lx + d[0], ly + d[1]) for d in (*DIRS, *FAR)}
    z_at, hi_at, core_at = gx // 4, lax.rem(gx // 2, 2), lax.rem(gx, 2)
    a_at = hi_at * 8 + gy
    b_at = z_at * 2 + core_at

    def a_device(t):
        to = lax.rem(a_at + t, 16)
        return (z_at * 4 + (to // 8) * 2 + core_at, lax.rem(to, 8))

    def b_device(t):
        to = lax.rem(b_at + t, 16)
        return ((to // 2) * 4 + hi_at * 2 + lax.rem(to, 2), gy)

    own = slice(HALO, HALO + BY)
    own_y = pl.ds(OY, BY)
    wide = pl.ds(Y0, COLS)

    def center(pack, f):
        return pack.at[1, pl.ds(f * BX, BX), pl.ds(HALO, BY), :]

    loads = []
    for source, target in (
        (boundary_hbm, boundary_in),
        (log_hbm, log_in),
        (material_hbm, material_home),
        (disp_hbm, disp_home),
    ):
        loads.append(pltpu.make_async_copy(source, target, load_sem.at[len(loads)]))
        loads[-1].start()

    barrier = pltpu.get_barrier_semaphore()
    for d in (*DIRS, *FAR):
        pl.semaphore_signal(barrier, inc=1, device_id=neighbours[d], device_id_type=MESH)
    for t in range(1, 16):
        pl.semaphore_signal(barrier, inc=1, device_id=a_device(t), device_id_type=MESH)
        pl.semaphore_signal(barrier, inc=1, device_id=b_device(t), device_id_type=MESH)

    @pl.when(moves)
    def _():
        pl.semaphore_signal(barrier, inc=1, device_id=host, device_id_type=MESH)
        pl.semaphore_signal(barrier, inc=1, device_id=home, device_id_type=MESH)

    lane = lax.broadcasted_iota(jnp.int32, (COLS, NZ), 1)
    col = lax.broadcasted_iota(jnp.int32, (COLS, NZ), 0) + (ly * BY - HALO)
    col_in = jnp.where((col >= 0) & (col < GY * BY), 1.0, 0.0)
    col_face = jnp.where((col >= 0) & (col + 1 < GY * BY), 0.5, 0.0)
    top_lane = lane == NZ - 1

    def row_in(i):
        at = lx * BX + (i - HALO)
        return jnp.where((at >= 0) & (at < GX * BX), 1.0, 0.0)

    loads[0].wait()
    kind = boundary_in[...]
    factor = jnp.where(kind == 1, 1.0, jnp.where(kind == 2, 4.0, 0.0)).astype(jnp.float32)
    diagonal_at = lax.broadcasted_iota(jnp.int32, (BY, BY), 0) == lax.broadcasted_iota(
        jnp.int32, (BY, BY), 1
    )
    tops = jnp.zeros((BY, NZ), jnp.float32)
    for r in range(BX):
        spread = jnp.broadcast_to(factor[r : r + 1, :], (BY, BY))
        column = jnp.sum(jnp.where(diagonal_at, spread, 0.0), axis=1, keepdims=True)
        tops = jnp.where(lane[:BY] == r, column, tops)
    tops_home[...] = tops
    for load in loads[1:4]:
        load.wait()
    for r in range(BX):
        material = material_home[r]
        base = jnp.zeros((BY, NZ), jnp.float32)
        for m in range(MATS):
            base = jnp.where(material == m, table_in[m], base)
        conductivity = base * jnp.exp(log_in[r])
        made[0, r] = conductivity
        made[1, r] = disp_home[r] * conductivity

    class Move:
        def __init__(self, source, target, sends, recvs, to):
            self.here = pltpu.make_async_copy(source, target, recvs)
            self.there = pltpu.make_async_remote_copy(
                src_ref=source,
                dst_ref=target,
                send_sem=sends,
                recv_sem=recvs,
                device_id=to,
                device_id_type=MESH,
            )

        def start(self):
            pl.when(stays)(self.here.start)
            pl.when(moves)(self.there.start)

        def arrive(self):
            pl.when(stays)(self.here.wait)
            pl.when(moves)(self.there.wait_recv)

        def wait_send(self):
            pl.when(moves)(self.there.wait_send)

    moved = []
    for source, target in (
        (made.at[0], center(first, 0)),
        (head_hbm, center(first, 1)),
        (source_hbm, center(first, 2)),
        (tops_home, first.at[1, 3 * BX, pl.ds(HALO, BY), :]),
        (made.at[1], center(second, 0)),
        (solute_weight_hbm, center(second, 1)),
        (solute_hbm, xe_solute.at[0, pl.ds(OX, BX), own_y, :]),
        (head_weight_hbm, head_weight_in),
        (material_hbm, material_in),
    ):
        k = len(moved)
        moved.append(Move(source, target, move_send.at[k], move_recv.at[k], host))

    pl.semaphore_wait(barrier, len(DIRS) + len(FAR) + 30 + jnp.where(stays, 0, 2))
    for move in moved[:6]:
        move.start()

    near = lax.broadcasted_iota(jnp.int32, (HALO, NZ), 0)

    def launch(event, d, source, target):
        k = DIRS.index(d)
        copy = pltpu.make_async_remote_copy(
            src_ref=source,
            dst_ref=target,
            send_sem=send_sem.at[event, k],
            recv_sem=recv_sem.at[event, k],
            device_id=neighbours[d],
            device_id_type=MESH,
        )
        copy.start()
        return copy

    def exchange(event, source_of, target_of, base, fields, extra=None):
        copies = [launch(event, d, source_of(d), target_of(d)) for d in FACES]
        parts = []
        for k, (dx, dy) in enumerate(CORNERS):
            at = base
            for radius, read, _ in fields:
                for d, partner, cells in CORNER_ROWS[radius]:
                    tile = read(d, dx, dy)
                    if partner is not None:
                        other = read(partner, dx, dy)
                        if dy > 0:
                            tile = jnp.where(near >= HALO - cells, tile, pltpu.roll(other, HALO - cells, 0))
                        else:
                            tile = jnp.where(near < cells, tile, pltpu.roll(other, cells, 0))
                    corner_out[k, at] = tile
                    at += 1
            if extra is not None:
                corner_out[k, at] = extra[0](dx, dy)
                at += 1
            parts.append(pl.ds(base, at - base))
        copies.extend(
            launch(event, d, corner_out.at[k, parts[k]], corner_in.at[k, parts[k]])
            for k, d in enumerate(CORNERS)
        )
        started.extend(copies)

        def lay():
            for k, (dx, dy) in enumerate(CORNERS):
                at = base
                for radius, _, write in fields:
                    for d, partner, cells in CORNER_ROWS[radius]:
                        tile = corner_in[k, at]
                        write(d, dx, dy, tile)
                        if partner is not None:
                            back = cells if dy > 0 else HALO - cells
                            write(partner, dx, dy, pltpu.roll(tile, back, 0))
                        at += 1
                if extra is not None:
                    extra[1](dx, dy, corner_in[k, at])

        return copies, lay

    def exchange_pack(event, pack, base, radii, extra=None):
        def source_of(d):
            first_col, size = y_from(d[1])
            return pack.at[1, :, pl.ds(HALO + first_col, size), :]

        def target_of(d):
            first_col, size = y_into(d[1])
            return pack.at[1 - d[0], :, pl.ds(first_col, size), :]

        def field(f, radius):
            def row(d, dx):
                return f * BX + (BX - d if dx > 0 else d - 1)

            def read(d, dx, dy):
                return pack[1, row(d, dx), pl.ds(HALO + y_from(dy)[0], HALO), :]

            def write(d, dx, dy, tile):
                pack[1 - dx, row(d, dx), pl.ds(y_into(dy)[0], HALO), :] = tile

            return radius, read, write

        fields = [field(f, radius) for f, radius in enumerate(radii)]
        if extra is not None:
            at = extra
            extra = (
                lambda dx, dy: pack[1, at, pl.ds(HALO + y_from(dy)[0], HALO), :],
                lambda dx, dy, tile: pack.__setitem__(
                    (1 - dx, at, pl.ds(y_into(dy)[0], HALO), slice(None)), tile
                ),
            )
        return exchange(event, source_of, target_of, base, fields, extra)

    def exchange_field(event, ref, base, *leads, faces=None):
        lead_all = faces or leads[0]

        def source_of(d):
            first_col, size = y_from(d[1])
            return ref.at[(*lead_all, pl.ds(OX, BX), pl.ds(OY + first_col, size), slice(None))]

        def target_of(d):
            first_col, size = y_into(d[1])
            part = x_part(d[0])
            rows = pl.ds(part.start, part.stop - part.start)
            return ref.at[(*lead_all, rows, pl.ds(Y0 + first_col, size), slice(None))]

        def field(lead):
            def read(d, dx, dy):
                row = OX + BX - d if dx > 0 else OX + d - 1
                return ref[(*lead, row, pl.ds(OY + y_from(dy)[0], HALO))]

            def write(d, dx, dy, tile):
                row = OX - d if dx > 0 else OX + BX - 1 + d
                ref[(*lead, row, pl.ds(Y0 + y_into(dy)[0], HALO))] = tile

            return HALO, read, write

        if base is None:
            copies = [launch(event, d, source_of(d), target_of(d)) for d in FACES]
            started.extend(copies)
            return copies, None
        return exchange(event, source_of, target_of, base, [field(lead) for lead in leads])

    def arrive(got):
        copies, lay = got
        for copy in copies:
            copy.wait_recv()
        if lay is not None:
            lay()

    def send_to(d, source, target, k):
        copy = pltpu.make_async_remote_copy(
            src_ref=source,
            dst_ref=target,
            send_sem=send_far.at[k],
            recv_sem=recv_far.at[k],
            device_id=neighbours[d],
            device_id_type=MESH,
        )
        copy.start()
        return copy

    started = []
    for move in moved[:4]:
        move.arrive()
    got_first = exchange_pack(0, first, 0, (8, 8, 8), 3 * BX)
    for move in moved[4:6]:
        move.arrive()
    got_second = exchange_pack(1, second, 13, (9, 8))
    rows = pl.ds(0, BX)
    got_far = [
        send_to((2, 0), second.at[1, BX - 1, pl.ds(HALO, BY), :], far_x.at[0], 0),
        send_to((-2, 0), second.at[1, 0, pl.ds(HALO, BY), :], far_x.at[1], 1),
        send_to((0, 1), second.at[1, rows, pl.ds(HALO, HALO), :], far_y.at[0], 2),
        send_to((0, -1), second.at[1, rows, pl.ds(BY, HALO), :], far_y.at[1], 3),
    ]
    started += got_far

    for move in moved[6:8]:
        move.start()

    at_low, at_high = col == ly * BY - HALO, col == ly * BY + BY + HALO - 1
    low_face = jnp.where(at_low & (col > 0) & (col < GY * BY), 0.5, 0.0)

    def coefficients(field, value_of, beyond):
        row = value_of(0)
        face_before = None
        if beyond:
            face_before = (value_of(-1) + row) * (0.5 * row_in(-1) * row_in(0))
        for i in range(ROWS):
            face = None
            if beyond or i + 1 < ROWS:
                ahead = value_of(i + 1)
                face = (row + ahead) * (0.5 * row_in(i) * row_in(i + 1))
                if i + 1 < ROWS:
                    cx[field, i] = face
            north = pltpu.roll(row, COLS - 1, 0)
            far = beyond and OX <= i < OX + BX
            if far:
                north = jnp.where(at_high, far_y[1, i - OX, 0:1, :], north)
            side = (row + north) * col_face
            cy[field, i, wide, :] = side
            layer = jnp.where(top_lane, 0.0, 0.5 * (row + up(row)))
            czu[field, i] = layer
            under = down(layer)
            if face is not None and face_before is not None:
                south = pltpu.roll(side, 1, 0)
                if far:
                    low = (row + far_y[0, i - OX, HALO - 1 : HALO, :]) * low_face
                    south = jnp.where(at_low, low, south)
                tile = first[i // BX, 3 * BX, :, :]
                top = jnp.where(top_lane, pltpu.roll(tile, NZ - 1 - i % BX, 1), 0.0)
                diag = 1.0 + face + face_before + side + south + layer + under + top * row
                inv[field, i] = (col_in * row_in(i)) / diag
            if face is not None:
                row, face_before = ahead, face

    def sweep(field, cur, nxt, lo, hi, right, y_at=0, y_size=COLS):
        here, span = pl.ds(Y0 + y_at, y_size), pl.ds(y_at, y_size)
        ahead, behind = pl.ds(Y0 + y_at + 1, y_size), pl.ds(Y0 + y_at - 1, y_size)
        west, mid = cur[lo - 1, here, :], cur[lo, here, :]
        face_west = cx[field, lo - 1, span, :]
        for i in range(lo, hi):
            east = cur[i + 1, here, :]
            face_east = cx[field, i, span, :]
            total = face_east * east + face_west * west
            total = total + cy[field, i, here, :] * cur[i, ahead, :]
            total = total + cy[field, i, behind, :] * cur[i, behind, :]
            layer = czu[field, i, span, :]
            total = total + layer * up(mid) + down(layer * mid)
            if right is not None:
                total = total + right[i, span, :]
            nxt[i, here, :] = total * inv[field, i, span, :]
            west, mid, face_west = mid, east, face_east

    def relax(right, base, *chains):
        def step(t, upward, lo, hi, *y):
            for field, even, odd in chains:
                if upward:
                    sweep(field, even.at[t], odd.at[t], lo, hi, right, *y)
                else:
                    sweep(field, odd.at[t], even.at[t + 1], lo, hi, right, *y)

        step(base, True, 1, ROWS - 1)
        step(base, False, 2, ROWS - 2)
        step(base + 1, True, 3, ROWS - 3)
        step(base + 1, False, 4, ROWS - 4)
        step(base + 2, True, 5, ROWS - 5)
        step(base + 2, False, 6, ROWS - 6)
        step(base + 3, True, 7, ROWS - 7)
        step(base + 3, False, OX, OX + BX, HALO, BY)

    def top_of(r):
        tile = first[1, 3 * BX, own, :]
        return jnp.where(lane[:BY] == NZ - 1, pltpu.roll(tile, NZ - 1 - r, 1), 0.0)

    def retrace(*pairs):
        relax(None, 0, *((field, lam_even.at[which], lam_odd.at[which]) for field, which in pairs))

    def right_bar(which, r):
        total = lam_even[which, 0, OX + r, own_y, :] + lam_odd[which, 0, OX + r, own_y, :]
        for k in range(1, 4):
            total = total + lam_even[which, k, OX + r, own_y, :]
            total = total + lam_odd[which, k, OX + r, own_y, :]
        return total

    acc_side[...] = jnp.zeros_like(acc_side)
    acc_layer[...] = jnp.zeros_like(acc_layer)
    acc_drop[...] = jnp.zeros_like(acc_drop)
    north_in = jnp.where(col[own] + 1 < GY * BY, 1.0, 0.0)
    south_in = jnp.where(col[own] > 0, 1.0, 0.0)
    east_in, west_in = row_in(OX + BX), row_in(OX - 1)

    def around(ref, lead, r):
        east, west = ref[(*lead, r + 1, own_y)], ref[(*lead, r - 1, own_y)]
        if r == OX + BX - 1:
            east = east * east_in
        if r == OX:
            west = west * west_in
        north = ref[(*lead, r, pl.ds(OY + 1, BY))] * north_in
        south = ref[(*lead, r, pl.ds(OY - 1, BY))] * south_in
        return east + west + north + south

    def gather(field, even, odd, base, which):
        def body(t, carry):
            steps = (
                ((lam_odd, (which, 3 - t)), (even, (base + t,))),
                ((lam_even, (which, 3 - t)), (odd, (base + t,))),
            )
            for r in range(OX, OX + BX):
                side = acc_side[field, r - OX]
                layer = acc_layer[field, r - OX]
                for (lam, at), (old, old_at) in steps:
                    lam_here = lam[(*at, r, own_y)]
                    old_here = old[(*old_at, r, own_y)]
                    side = side + lam_here * around(old, old_at, r)
                    side = side + old_here * around(lam, at, r)
                    layer = layer + lam_here * up(old_here) + old_here * up(lam_here)
                acc_side[field, r - OX] = side
                acc_layer[field, r - OX] = layer
            return carry

        lax.fori_loop(0, 4, body, 0)

    def drops(field, *products):
        for r in range(OX - 1, OX + BX + 1):
            drop = acc_drop[field, r - OX + 1, wide, :]
            for (lam, at), (new, new_at) in products:
                drop = drop + lam[(*at, r, wide)] * new[(*new_at, r, wide)]
            acc_drop[field, r - OX + 1, wide, :] = drop

    def last_drop(field, even, base, which):
        drops(field, ((lam_even, (which, 0)), (even, (base + 4,))))

    def gather_drop(field, even, odd, base, which):
        def body(t, carry):
            drops(
                field,
                ((lam_odd, (which, 3 - t)), (odd, (base + t,))),
                ((lam_even, (which, 3 - t)), (even, (base + t + 1,))),
            )
            return carry

        lax.fori_loop(0, 3, body, 0)
        drops(field, ((lam_odd, (which, 0)), (odd, (base + 3,))))

    arrive(got_first)
    coefficients(HEAD, lambda i: first[i // BX, i % BX, :, :], False)
    for i in range(ROWS):
        start = first[i // BX, BX + i % BX, :, :]
        xe_head[0, i, wide, :] = start
        rhs[i] = start + first[i // BX, 2 * BX + i % BX, :, :]
    relax(rhs, 0, (HEAD, xe_head, xo_head))
    got_head1 = exchange_field(3, xe_head, 26, (4,))
    moved[8].start()
    moved[6].arrive()
    got_start = exchange_field(2, xe_solute, 22, (0,))

    arrive(got_second)
    arrive((got_far, None))

    def spreading(i):
        if 0 <= i < ROWS:
            return second[i // BX, i % BX, :, :]
        beyond = far_x[0 if i < 0 else 1]
        return jnp.concatenate([beyond[:HALO], beyond, beyond[:HALO]], axis=0)

    coefficients(SOLUTE, spreading, True)
    for i in range(ROWS):
        lam_even[0, 0, i, wide, :] = second[i // BX, BX + i % BX, :, :] * inv[SOLUTE, i]
    retrace((SOLUTE, 0))
    moved[7].arrive()
    for r in range(BX):
        bar = right_bar(0, r)
        lam_even[1, 0, OX + r, own_y, :] = (head_weight_in[r] + coupling_rate * bar) * inv[
            HEAD, OX + r, own, :
        ]
        lam_even[2, 0, OX + r, own_y, :] = (
            lam_even[0, 4, OX + r, own_y, :] + bar * inv[SOLUTE, OX + r, own, :]
        )
    got_lam_mid = exchange_field(4, lam_even, 30, (1, 0), (2, 0), faces=(pl.ds(1, 2), 0))

    arrive(got_head1)
    for i in range(ROWS):
        rhs[i] = xe_head[4, i, wide, :] + first[i // BX, 2 * BX + i % BX, :, :]
    relax(rhs, 4, (HEAD, xe_head, xo_head))
    got_head2 = exchange_field(5, xe_head, 38, (8,))
    arrive(got_start)
    for i in range(ROWS):
        rhs[i] = xe_solute[0, i, wide, :] + coupling_rate * xe_head[4, i, wide, :]
    relax(rhs, 0, (SOLUTE, xe_solute, xo_solute))
    got_solute1 = exchange_field(6, xe_solute, 42, (4,))
    arrive(got_lam_mid)
    retrace((HEAD, 1), (SOLUTE, 2))
    for r in range(BX):
        bar = right_bar(1, r) + coupling_rate * right_bar(2, r)
        lam_even[3, 0, OX + r, own_y, :] = (
            lam_even[1, 4, OX + r, own_y, :] + bar * inv[HEAD, OX + r, own, :]
        )
    got_lam_h1 = exchange_field(7, lam_even, 46, (3, 0))

    gather(HEAD, xe_head, xo_head, 4, 1)
    gather_drop(HEAD, xe_head, xo_head, 4, 1)
    gather(SOLUTE, xe_solute, xo_solute, 0, 2)
    gather_drop(SOLUTE, xe_solute, xo_solute, 0, 2)

    arrive(got_head2)
    arrive(got_solute1)
    for i in range(ROWS):
        rhs[i] = xe_solute[4, i, wide, :] + coupling_rate * xe_head[8, i, wide, :]
    relax(rhs, 4, (SOLUTE, xe_solute, xo_solute))
    got_solute2 = exchange_field(8, xe_solute, None, (8,))
    stores = []

    def hand_out(source, k):
        stores.append(Move(source, fields_out.at[k], store_send.at[k], store_sem.at[k], home))
        stores[-1].start()

    hand_out(xe_head.at[8, pl.ds(OX, BX), own_y, :], 0)
    hand_out(xe_solute.at[8, pl.ds(OX, BX), own_y, :], 1)
    arrive(got_lam_h1)
    retrace((HEAD, 3))
    gather(HEAD, xe_head, xo_head, 0, 3)
    gather_drop(HEAD, xe_head, xo_head, 0, 3)
    last_drop(HEAD, xe_head, 0, 3)
    last_drop(HEAD, xe_head, 4, 1)
    last_drop(SOLUTE, xe_solute, 0, 2)
    gather(SOLUTE, xe_solute, xo_solute, 4, 0)
    gather_drop(SOLUTE, xe_solute, xo_solute, 4, 0)
    arrive(got_solute2)
    last_drop(SOLUTE, xe_solute, 4, 0)

    for move in moved[8:]:
        move.arrive()
    own_lane = lane[:BY]
    inner_top = own_lane < NZ - 1
    inner_low = own_lane > 0

    def sensitivity(field, r):
        layer = jnp.where(inner_top, acc_layer[field, r], 0.0)
        drop = acc_drop[field, r + 1, own_y, :]
        east, west = acc_drop[field, r + 2, own_y, :], acc_drop[field, r, own_y, :]
        count = north_in + south_in
        if r == BX - 1:
            east = east * east_in
        if r == 0:
            west = west * west_in
        count = count + (east_in if r == BX - 1 else 1.0) + (west_in if r == 0 else 1.0)
        count = count + jnp.where(inner_top, 1.0, 0.0) + jnp.where(inner_low, 1.0, 0.0)
        total = acc_side[field, r] + layer + down(layer) - count * drop - east - west
        total = total - acc_drop[field, r + 1, pl.ds(OY + 1, BY), :] * north_in
        total = total - acc_drop[field, r + 1, pl.ds(OY - 1, BY), :] * south_in
        total = total - jnp.where(inner_top, up(drop), 0.0) - jnp.where(inner_low, down(drop), 0.0)
        return 0.5 * total - top_of(r) * drop

    sums = [jnp.zeros((BY, NZ), jnp.float32) for _ in range(MATS)]
    for r in range(BX):
        conductivity = first[1, r, own, :]
        spread_bar = sensitivity(SOLUTE, r)
        dispersivity = second[1, r, own, :] / conductivity
        total_bar = sensitivity(HEAD, r) + dispersivity * spread_bar
        scaled = total_bar * conductivity
        grads[0, r] = scaled
        grads[1, r] = spread_bar * conductivity
        material = material_in[r]
        for m in range(MATS):
            sums[m] = sums[m] + jnp.where(material == m, scaled, 0.0)
    hand_out(grads.at[0], 2)
    hand_out(grads.at[1], 3)
    mat_row = lax.broadcasted_iota(jnp.int32, (MATS, NZ), 0)
    partial = jnp.zeros((MATS, NZ), jnp.float32)
    for m in range(MATS):
        partial = jnp.where(mat_row == m, jnp.sum(sums[m], axis=0, keepdims=True), partial)
    mat_lane = lax.broadcasted_iota(jnp.int32, (MATS, NZ), 1)
    partial = jnp.sum(partial, axis=1, keepdims=True)
    partial = jnp.sum(jnp.where(mat_row == mat_lane, partial, 0.0), axis=0, keepdims=True)

    def reduce(part, at, device_of, sends, recvs, value):
        part[at] = value
        copies = []
        for t in range(1, 16):
            copies.append(
                pltpu.make_async_remote_copy(
                    src_ref=part.at[at],
                    dst_ref=part.at[at],
                    send_sem=sends.at[t],
                    recv_sem=recvs.at[t],
                    device_id=device_of(t),
                    device_id_type=MESH,
                )
            )
            copies[-1].start()
        for t in range(1, 16):
            slot = lax.rem(at - t + 16, 16)
            pltpu.make_async_remote_copy(
                src_ref=part.at[slot],
                dst_ref=part.at[slot],
                send_sem=sends.at[t],
                recv_sem=recvs.at[t],
                device_id=device_of(t),
                device_id_type=MESH,
            ).wait_recv()
        total = part[0]
        for k in range(1, 16):
            total = total + part[k]
        return copies, total

    copies, partial = reduce(part_a, a_at, a_device, send_a, recv_a, partial)
    started += copies
    copies, partial = reduce(part_b, b_at, b_device, send_b, recv_b, partial)
    started += copies
    base = jnp.ones((1, NZ), jnp.float32)
    for m in range(MATS):
        base = jnp.where(lane[:1] == m, table_in[m], base)
    grad_table_out[...] = partial / base
    for copy in started:
        copy.wait_send()
    for store in stores:
        store.arrive()
    for move in moved + stores:
        move.wait_send()


def hand_over(fields, table, head_out, solute_out, grad_cond_out, grad_disp_out, grad_table_out):
    for k, out in enumerate((head_out, solute_out, grad_cond_out, grad_disp_out)):
        out[...] = fields[k]
    for m in range(MATS):
        grad_table_out[m] = table[0, m]


def local(*arrays):
    f32 = jnp.float32
    block = jax.ShapeDtypeStruct((BX, BY, NZ), f32)
    vmem = pl.BlockSpec(memory_space=pltpu.VMEM)
    smem = pl.BlockSpec(memory_space=pltpu.SMEM)
    anywhere = pl.BlockSpec(memory_space=pl.ANY)
    fields, table = pl.pallas_call(
        kernel,
        out_shape=(
            jax.ShapeDtypeStruct((4, BX, BY, NZ), f32),
            jax.ShapeDtypeStruct((1, NZ), f32),
        ),
        in_specs=[smem if k == 6 else anywhere for k in range(10)],
        out_specs=(anywhere, vmem),
        scratch_shapes=[
            pltpu.VMEM((BX, BY, NZ), f32),
            pltpu.VMEM((BX, BY, NZ), jnp.int32),
            pltpu.VMEM((BX, BY), jnp.int32),
            pltpu.VMEM((BX, BY, NZ), f32),
            pltpu.VMEM((2, BX, BY, NZ), f32),
            pltpu.VMEM((BX, BY, NZ), jnp.int32),
            pltpu.VMEM((BX, BY, NZ), f32),
            pltpu.VMEM((2, BX, BY, NZ), f32),
            pltpu.VMEM((BY, NZ), f32),
            pltpu.SemaphoreType.DMA((4,)),
            pltpu.SemaphoreType.DMA((4,)),
            pltpu.SemaphoreType.DMA((4,)),
            pltpu.SemaphoreType.DMA((10,)),
            pltpu.SemaphoreType.DMA((10,)),
            pltpu.VMEM((3, 3 * BX + 1, COLS, NZ), f32),
            pltpu.VMEM((3, 2 * BX, COLS, NZ), f32),
            pltpu.VMEM((2, BY, NZ), f32),
            pltpu.VMEM((2, BX, HALO, NZ), f32),
            pltpu.VMEM((4, TILES, HALO, NZ), f32),
            pltpu.VMEM((4, TILES, HALO, NZ), f32),
            pltpu.VMEM((2, ROWS, COLS, NZ), f32),
            pltpu.VMEM((2, ROWS, PAD, NZ), f32),
            pltpu.VMEM((2, ROWS, COLS, NZ), f32),
            pltpu.VMEM((2, ROWS, COLS, NZ), f32),
            pltpu.VMEM((ROWS, COLS, NZ), f32),
            pltpu.VMEM((9, ROWS, PAD, NZ), f32),
            pltpu.VMEM((8, ROWS, PAD, NZ), f32),
            pltpu.VMEM((9, ROWS, PAD, NZ), f32),
            pltpu.VMEM((8, ROWS, PAD, NZ), f32),
            pltpu.VMEM((4, 5, ROWS, PAD, NZ), f32),
            pltpu.VMEM((4, 4, ROWS, PAD, NZ), f32),
            pltpu.VMEM((2, BX, BY, NZ), f32),
            pltpu.VMEM((2, BX, BY, NZ), f32),
            pltpu.VMEM((2, BX + 2, PAD, NZ), f32),
            pltpu.VMEM((16, 1, NZ), f32),
            pltpu.VMEM((16, 1, NZ), f32),
            pltpu.SemaphoreType.DMA((9, 8)),
            pltpu.SemaphoreType.DMA((9, 8)),
            pltpu.SemaphoreType.DMA((4,)),
            pltpu.SemaphoreType.DMA((4,)),
            pltpu.SemaphoreType.DMA((16,)),
            pltpu.SemaphoreType.DMA((16,)),
            pltpu.SemaphoreType.DMA((16,)),
            pltpu.SemaphoreType.DMA((16,)),
        ],
        compiler_params=pltpu.CompilerParams(
            collective_id=0, has_side_effects=True, vmem_limit_bytes=58 << 20
        ),
        name="window",
    )(*arrays)
    return pl.pallas_call(
        hand_over,
        out_shape=(block, block, block, block, jax.ShapeDtypeStruct((MATS,), f32)),
        in_specs=[vmem, vmem],
        out_specs=(vmem,) * 4 + (smem,),
        name="hand_over",
    )(fields, table)


def solution(mesh):
    block = P("gx", "gy", None)
    return jax.shard_map(
        local,
        mesh=mesh,
        in_specs=(block, block, block, block, block, block, P(), P("gx", "gy"), block, block),
        out_specs=(block, block, block, block, P()),
        check_vma=False,
    )
```

```python
import jax
import jax.numpy as jnp
from jax import lax
from jax.experimental import pallas as pl
from jax.experimental.pallas import tpu as pltpu
from jax.sharding import PartitionSpec as P

SWEEPS = 8
MATS = 8
coupling_rate = 0.5

BX, BY, NZ, HALO = 8, 16, 128, 8
GX, GY = 32, 8
ROWS = BX + 2 * HALO
COLS = BY + 2 * HALO
PAD = COLS + 16
Y0, Y1 = 8, 8 + COLS
OX, OY = HALO, 8 + HALO
MESH = pl.DeviceIdType.MESH
DIRS = ((1, 0), (-1, 0), (0, 1), (0, -1), (1, 1), (1, -1), (-1, 1), (-1, -1))
FAR = ((2, 0), (-2, 0))
FACES, CORNERS = DIRS[:4], DIRS[4:]
TILES = 50
HEAD, SOLUTE = 0, 1


def host_of(bx, by):
    z, half = bx // 4, by // 4
    pair = lax.rem(lax.rem(bx // 2, 2) + z, 2)
    x = jnp.where(half == 0, pair, 3 - pair)
    y = jnp.where(half == 0, lax.rem(by, 4), 3 - lax.rem(by, 4))
    return (z * 4 + (x // 2) * 2 + lax.rem(bx, 2), lax.rem(x, 2) * 4 + y)


def block_of(gx, gy):
    z, x, y = gx // 4, lax.rem(gx // 2, 2) * 2 + gy // 4, lax.rem(gy, 4)
    half = x // 2
    pair = jnp.where(half == 0, x, 3 - x)
    high = lax.rem(pair + z, 2)
    return (z * 4 + high * 2 + lax.rem(gx, 2), half * 4 + jnp.where(half == 0, y, 3 - y))


def place(bx, by):
    return host_of(lax.rem(bx + GX, GX), lax.rem(by + GY, GY))


def x_part(dx):
    return {0: slice(OX, OX + BX), 1: slice(0, HALO), -1: slice(OX + BX, ROWS)}[dx]


def y_from(dy):
    return {0: (0, BY), 1: (BY - HALO, HALO), -1: (0, HALO)}[dy]


def y_into(dy):
    return {0: (HALO, BY), 1: (0, HALO), -1: (HALO + BY, HALO)}[dy]


CORNER_ROWS = {
    8: ((1, 7, 7), (2, 6, 6), (3, 5, 5), (4, None, 4)),
    9: ((1, None, 8), (2, 8, 7), (3, 7, 6), (4, 6, 5), (5, None, 4)),
}


def up(cells):
    return pltpu.roll(cells, NZ - 1, 1)


def down(cells):
    return pltpu.roll(cells, 1, 1)


def kernel(
    head_hbm,
    solute_hbm,
    source_hbm,
    log_hbm,
    disp_hbm,
    material_hbm,
    table_in,
    boundary_hbm,
    head_weight_hbm,
    solute_weight_hbm,
    fields_out,
    grad_table_out,
    log_in,
    material_in,
    boundary_in,
    head_weight_in,
    grads,
    material_home,
    disp_home,
    made,
    tops_home,
    load_sem,
    store_sem,
    store_send,
    move_send,
    move_recv,
    first,
    second,
    far_x,
    far_y,
    corner_out,
    corner_in,
    cx,
    cy,
    czu,
    inv,
    rhs,
    xe_head,
    xo_head,
    xe_solute,
    xo_solute,
    lam_even,
    lam_odd,
    acc_side,
    acc_layer,
    acc_drop,
    part_a,
    part_b,
    send_sem,
    recv_sem,
    send_far,
    recv_far,
    send_a,
    recv_a,
    send_b,
    recv_b,
):
    gx, gy = lax.axis_index("gx"), lax.axis_index("gy")
    lx, ly = block_of(gx, gy)
    host, home = host_of(gx, gy), (lx, ly)
    stays = (lx == gx) & (ly == gy)
    moves = jnp.logical_not(stays)
    neighbours = {d: place(lx + d[0], ly + d[1]) for d in (*DIRS, *FAR)}
    z_at, hi_at, core_at = gx // 4, lax.rem(gx // 2, 2), lax.rem(gx, 2)
    a_at = hi_at * 8 + gy
    b_at = z_at * 2 + core_at

    def a_device(t):
        to = lax.rem(a_at + t, 16)
        return (z_at * 4 + (to // 8) * 2 + core_at, lax.rem(to, 8))

    def b_device(t):
        to = lax.rem(b_at + t, 16)
        return ((to // 2) * 4 + hi_at * 2 + lax.rem(to, 2), gy)

    own = slice(HALO, HALO + BY)
    own_y = pl.ds(OY, BY)
    wide = pl.ds(Y0, COLS)

    def center(pack, f):
        return pack.at[1, pl.ds(f * BX, BX), pl.ds(HALO, BY), :]

    loads = []
    for source, target in (
        (boundary_hbm, boundary_in),
        (log_hbm, log_in),
        (material_hbm, material_home),
        (disp_hbm, disp_home),
    ):
        loads.append(pltpu.make_async_copy(source, target, load_sem.at[len(loads)]))
        loads[-1].start()

    barrier = pltpu.get_barrier_semaphore()
    for d in (*DIRS, *FAR):
        pl.semaphore_signal(barrier, inc=1, device_id=neighbours[d], device_id_type=MESH)
    for t in range(1, 16):
        pl.semaphore_signal(barrier, inc=1, device_id=a_device(t), device_id_type=MESH)
        pl.semaphore_signal(barrier, inc=1, device_id=b_device(t), device_id_type=MESH)

    @pl.when(moves)
    def _():
        pl.semaphore_signal(barrier, inc=1, device_id=host, device_id_type=MESH)
        pl.semaphore_signal(barrier, inc=1, device_id=home, device_id_type=MESH)

    lane = lax.broadcasted_iota(jnp.int32, (COLS, NZ), 1)
    col = lax.broadcasted_iota(jnp.int32, (COLS, NZ), 0) + (ly * BY - HALO)
    col_in = jnp.where((col >= 0) & (col < GY * BY), 1.0, 0.0)
    col_face = jnp.where((col >= 0) & (col + 1 < GY * BY), 0.5, 0.0)
    top_lane = lane == NZ - 1

    def row_in(i):
        at = lx * BX + (i - HALO)
        return jnp.where((at >= 0) & (at < GX * BX), 1.0, 0.0)

    loads[0].wait()
    kind = boundary_in[...]
    factor = jnp.where(kind == 1, 1.0, jnp.where(kind == 2, 4.0, 0.0)).astype(jnp.float32)
    diagonal_at = lax.broadcasted_iota(jnp.int32, (BY, BY), 0) == lax.broadcasted_iota(
        jnp.int32, (BY, BY), 1
    )
    tops = jnp.zeros((BY, NZ), jnp.float32)
    for r in range(BX):
        spread = jnp.broadcast_to(factor[r : r + 1, :], (BY, BY))
        column = jnp.sum(jnp.where(diagonal_at, spread, 0.0), axis=1, keepdims=True)
        tops = jnp.where(lane[:BY] == r, column, tops)
    tops_home[...] = tops
    for load in loads[1:4]:
        load.wait()
    for r in range(BX):
        material = material_home[r]
        base = jnp.zeros((BY, NZ), jnp.float32)
        for m in range(MATS):
            base = jnp.where(material == m, table_in[m], base)
        conductivity = base * jnp.exp(log_in[r])
        made[0, r] = conductivity
        made[1, r] = disp_home[r] * conductivity

    class Move:
        def __init__(self, source, target, sends, recvs, to):
            self.here = pltpu.make_async_copy(source, target, recvs)
            self.there = pltpu.make_async_remote_copy(
                src_ref=source,
                dst_ref=target,
                send_sem=sends,
                recv_sem=recvs,
                device_id=to,
                device_id_type=MESH,
            )

        def start(self):
            pl.when(stays)(self.here.start)
            pl.when(moves)(self.there.start)

        def arrive(self):
            pl.when(stays)(self.here.wait)
            pl.when(moves)(self.there.wait_recv)

        def wait_send(self):
            pl.when(moves)(self.there.wait_send)

    moved = []
    for source, target in (
        (made.at[0], center(first, 0)),
        (head_hbm, center(first, 1)),
        (source_hbm, center(first, 2)),
        (tops_home, first.at[1, 3 * BX, pl.ds(HALO, BY), :]),
        (made.at[1], center(second, 0)),
        (solute_weight_hbm, center(second, 1)),
        (solute_hbm, xe_solute.at[0, pl.ds(OX, BX), own_y, :]),
        (head_weight_hbm, head_weight_in),
        (material_hbm, material_in),
    ):
        k = len(moved)
        moved.append(Move(source, target, move_send.at[k], move_recv.at[k], host))

    pl.semaphore_wait(barrier, len(DIRS) + len(FAR) + 30 + jnp.where(stays, 0, 2))
    for move in moved[:6]:
        move.start()

    near = lax.broadcasted_iota(jnp.int32, (HALO, NZ), 0)

    def launch(event, d, source, target):
        k = DIRS.index(d)
        copy = pltpu.make_async_remote_copy(
            src_ref=source,
            dst_ref=target,
            send_sem=send_sem.at[event, k],
            recv_sem=recv_sem.at[event, k],
            device_id=neighbours[d],
            device_id_type=MESH,
        )
        copy.start()
        return copy

    def exchange(event, source_of, target_of, base, fields, extra=None):
        copies = []
        late = len(fields) == 1
        if not late:
            copies.extend(launch(event, d, source_of(d), target_of(d)) for d in FACES)
        parts = []
        for k, (dx, dy) in enumerate(CORNERS):
            at = base
            for radius, read, _ in fields:
                for d, partner, cells in CORNER_ROWS[radius]:
                    tile = read(d, dx, dy)
                    if partner is not None:
                        other = read(partner, dx, dy)
                        if dy > 0:
                            tile = jnp.where(near >= HALO - cells, tile, pltpu.roll(other, HALO - cells, 0))
                        else:
                            tile = jnp.where(near < cells, tile, pltpu.roll(other, cells, 0))
                    corner_out[k, at] = tile
                    at += 1
            if extra is not None:
                corner_out[k, at] = extra[0](dx, dy)
                at += 1
            parts.append(pl.ds(base, at - base))
        copies.extend(
            launch(event, d, corner_out.at[k, parts[k]], corner_in.at[k, parts[k]])
            for k, d in enumerate(CORNERS)
        )
        if late:
            copies.extend(launch(event, d, source_of(d), target_of(d)) for d in FACES)
        started.extend(copies)

        def lay():
            for k, (dx, dy) in enumerate(CORNERS):
                at = base
                for radius, _, write in fields:
                    for d, partner, cells in CORNER_ROWS[radius]:
                        tile = corner_in[k, at]
                        write(d, dx, dy, tile)
                        if partner is not None:
                            back = cells if dy > 0 else HALO - cells
                            write(partner, dx, dy, pltpu.roll(tile, back, 0))
                        at += 1
                if extra is not None:
                    extra[1](dx, dy, corner_in[k, at])

        return copies, lay

    def exchange_pack(event, pack, base, radii, extra=None):
        def source_of(d):
            first_col, size = y_from(d[1])
            return pack.at[1, :, pl.ds(HALO + first_col, size), :]

        def target_of(d):
            first_col, size = y_into(d[1])
            return pack.at[1 - d[0], :, pl.ds(first_col, size), :]

        def field(f, radius):
            def row(d, dx):
                return f * BX + (BX - d if dx > 0 else d - 1)

            def read(d, dx, dy):
                return pack[1, row(d, dx), pl.ds(HALO + y_from(dy)[0], HALO), :]

            def write(d, dx, dy, tile):
                pack[1 - dx, row(d, dx), pl.ds(y_into(dy)[0], HALO), :] = tile

            return radius, read, write

        fields = [field(f, radius) for f, radius in enumerate(radii)]
        if extra is not None:
            at = extra
            extra = (
                lambda dx, dy: pack[1, at, pl.ds(HALO + y_from(dy)[0], HALO), :],
                lambda dx, dy, tile: pack.__setitem__(
                    (1 - dx, at, pl.ds(y_into(dy)[0], HALO), slice(None)), tile
                ),
            )
        return exchange(event, source_of, target_of, base, fields, extra)

    def exchange_field(event, ref, base, *leads, faces=None):
        lead_all = faces or leads[0]

        def source_of(d):
            first_col, size = y_from(d[1])
            return ref.at[(*lead_all, pl.ds(OX, BX), pl.ds(OY + first_col, size), slice(None))]

        def target_of(d):
            first_col, size = y_into(d[1])
            part = x_part(d[0])
            rows = pl.ds(part.start, part.stop - part.start)
            return ref.at[(*lead_all, rows, pl.ds(Y0 + first_col, size), slice(None))]

        def field(lead):
            def read(d, dx, dy):
                row = OX + BX - d if dx > 0 else OX + d - 1
                return ref[(*lead, row, pl.ds(OY + y_from(dy)[0], HALO))]

            def write(d, dx, dy, tile):
                row = OX - d if dx > 0 else OX + BX - 1 + d
                ref[(*lead, row, pl.ds(Y0 + y_into(dy)[0], HALO))] = tile

            return HALO, read, write

        if base is None:
            copies = []
            for dx, dy in FACES:
                source, target = source_of((dx, dy)), target_of((dx, dy))
                if dx != 0:
                    edge, beyond = (OX + BX - 1, OX - 1) if dx > 0 else (OX, OX + BX)
                    source = ref.at[(*lead_all, edge, own_y, slice(None))]
                    target = ref.at[(*lead_all, beyond, own_y, slice(None))]
                copies.append(launch(event, (dx, dy), source, target))
            started.extend(copies)
            return copies, None
        return exchange(event, source_of, target_of, base, [field(lead) for lead in leads])

    def arrive(got):
        copies, lay = got
        for copy in copies:
            copy.wait_recv()
        if lay is not None:
            lay()

    def send_to(d, source, target, k):
        copy = pltpu.make_async_remote_copy(
            src_ref=source,
            dst_ref=target,
            send_sem=send_far.at[k],
            recv_sem=recv_far.at[k],
            device_id=neighbours[d],
            device_id_type=MESH,
        )
        copy.start()
        return copy

    started = []
    for move in moved[:4]:
        move.arrive()
    got_first = exchange_pack(0, first, 0, (8, 8, 8), 3 * BX)
    for move in moved[4:6]:
        move.arrive()
    got_second = exchange_pack(1, second, 13, (9, 8))
    rows = pl.ds(0, BX)
    got_far = [
        send_to((2, 0), second.at[1, BX - 1, pl.ds(HALO, BY), :], far_x.at[0], 0),
        send_to((-2, 0), second.at[1, 0, pl.ds(HALO, BY), :], far_x.at[1], 1),
        send_to((0, 1), second.at[1, rows, pl.ds(HALO, HALO), :], far_y.at[0], 2),
        send_to((0, -1), second.at[1, rows, pl.ds(BY, HALO), :], far_y.at[1], 3),
    ]
    started += got_far

    for move in moved[6:8]:
        move.start()

    at_low, at_high = col == ly * BY - HALO, col == ly * BY + BY + HALO - 1
    low_face = jnp.where(at_low & (col > 0) & (col < GY * BY), 0.5, 0.0)

    def coefficients(field, value_of, beyond):
        row = value_of(0)
        face_before = None
        if beyond:
            face_before = (value_of(-1) + row) * (0.5 * row_in(-1) * row_in(0))
        for i in range(ROWS):
            face = None
            if beyond or i + 1 < ROWS:
                ahead = value_of(i + 1)
                face = (row + ahead) * (0.5 * row_in(i) * row_in(i + 1))
                if i + 1 < ROWS:
                    cx[field, i] = face
            north = pltpu.roll(row, COLS - 1, 0)
            far = beyond and OX <= i < OX + BX
            if far:
                north = jnp.where(at_high, far_y[1, i - OX, 0:1, :], north)
            side = (row + north) * col_face
            cy[field, i, wide, :] = side
            layer = jnp.where(top_lane, 0.0, 0.5 * (row + up(row)))
            czu[field, i] = layer
            under = down(layer)
            if face is not None and face_before is not None:
                south = pltpu.roll(side, 1, 0)
                if far:
                    low = (row + far_y[0, i - OX, HALO - 1 : HALO, :]) * low_face
                    south = jnp.where(at_low, low, south)
                tile = first[i // BX, 3 * BX, :, :]
                top = jnp.where(top_lane, pltpu.roll(tile, NZ - 1 - i % BX, 1), 0.0)
                diag = 1.0 + face + face_before + side + south + layer + under + top * row
                inv[field, i] = (col_in * row_in(i)) / diag
            if face is not None:
                row, face_before = ahead, face

    def sweep(field, cur, nxt, lo, hi, right, y_at=0, y_size=COLS):
        here, span = pl.ds(Y0 + y_at, y_size), pl.ds(y_at, y_size)
        ahead, behind = pl.ds(Y0 + y_at + 1, y_size), pl.ds(Y0 + y_at - 1, y_size)
        west, mid = cur[lo - 1, here, :], cur[lo, here, :]
        face_west = cx[field, lo - 1, span, :]
        for i in range(lo, hi):
            east = cur[i + 1, here, :]
            face_east = cx[field, i, span, :]
            total = face_east * east + face_west * west
            total = total + cy[field, i, here, :] * cur[i, ahead, :]
            total = total + cy[field, i, behind, :] * cur[i, behind, :]
            layer = czu[field, i, span, :]
            total = total + layer * up(mid) + down(layer * mid)
            if right is not None:
                total = total + right[i, span, :]
            nxt[i, here, :] = total * inv[field, i, span, :]
            west, mid, face_west = mid, east, face_east

    def relax(right, base, *chains):
        def step(t, upward, lo, hi, *y):
            for field, even, odd in chains:
                if upward:
                    sweep(field, even.at[t], odd.at[t], lo, hi, right, *y)
                else:
                    sweep(field, odd.at[t], even.at[t + 1], lo, hi, right, *y)

        step(base, True, 1, ROWS - 1)
        step(base, False, 2, ROWS - 2)
        step(base + 1, True, 3, ROWS - 3)
        step(base + 1, False, 4, ROWS - 4)
        step(base + 2, True, 5, ROWS - 5)
        step(base + 2, False, 6, ROWS - 6)
        step(base + 3, True, 7, ROWS - 7)
        step(base + 3, False, OX, OX + BX, HALO, BY)

    def top_of(r):
        tile = first[1, 3 * BX, own, :]
        return jnp.where(lane[:BY] == NZ - 1, pltpu.roll(tile, NZ - 1 - r, 1), 0.0)

    def retrace(*pairs):
        relax(None, 0, *((field, lam_even.at[which], lam_odd.at[which]) for field, which in pairs))

    def right_bar(which, r):
        total = lam_even[which, 0, OX + r, own_y, :] + lam_odd[which, 0, OX + r, own_y, :]
        for k in range(1, 4):
            total = total + lam_even[which, k, OX + r, own_y, :]
            total = total + lam_odd[which, k, OX + r, own_y, :]
        return total

    acc_side[...] = jnp.zeros_like(acc_side)
    acc_layer[...] = jnp.zeros_like(acc_layer)
    acc_drop[...] = jnp.zeros_like(acc_drop)
    north_in = jnp.where(col[own] + 1 < GY * BY, 1.0, 0.0)
    south_in = jnp.where(col[own] > 0, 1.0, 0.0)
    east_in, west_in = row_in(OX + BX), row_in(OX - 1)

    def around(ref, lead, r):
        east, west = ref[(*lead, r + 1, own_y)], ref[(*lead, r - 1, own_y)]
        if r == OX + BX - 1:
            east = east * east_in
        if r == OX:
            west = west * west_in
        north = ref[(*lead, r, pl.ds(OY + 1, BY))] * north_in
        south = ref[(*lead, r, pl.ds(OY - 1, BY))] * south_in
        return east + west + north + south

    def gather(field, even, odd, base, which):
        def body(t, carry):
            steps = (
                ((lam_odd, (which, 3 - t)), (even, (base + t,))),
                ((lam_even, (which, 3 - t)), (odd, (base + t,))),
            )
            for r in range(OX, OX + BX):
                side = acc_side[field, r - OX]
                layer = acc_layer[field, r - OX]
                for (lam, at), (old, old_at) in steps:
                    lam_here = lam[(*at, r, own_y)]
                    old_here = old[(*old_at, r, own_y)]
                    side = side + lam_here * around(old, old_at, r)
                    side = side + old_here * around(lam, at, r)
                    layer = layer + lam_here * up(old_here) + old_here * up(lam_here)
                acc_side[field, r - OX] = side
                acc_layer[field, r - OX] = layer
            return carry

        lax.fori_loop(0, 4, body, 0)

    def drops(field, *products):
        for r in range(OX - 1, OX + BX + 1):
            drop = acc_drop[field, r - OX + 1, wide, :]
            for (lam, at), (new, new_at) in products:
                drop = drop + lam[(*at, r, wide)] * new[(*new_at, r, wide)]
            acc_drop[field, r - OX + 1, wide, :] = drop

    def last_drop(field, even, base, which):
        drops(field, ((lam_even, (which, 0)), (even, (base + 4,))))

    def gather_drop(field, even, odd, base, which):
        def body(t, carry):
            drops(
                field,
                ((lam_odd, (which, 3 - t)), (odd, (base + t,))),
                ((lam_even, (which, 3 - t)), (even, (base + t + 1,))),
            )
            return carry

        lax.fori_loop(0, 3, body, 0)
        drops(field, ((lam_odd, (which, 0)), (odd, (base + 3,))))

    moved[6].arrive()
    got_start = exchange_field(2, xe_solute, 22, (0,))
    arrive(got_first)
    coefficients(HEAD, lambda i: first[i // BX, i % BX, :, :], False)
    for i in range(ROWS):
        start = first[i // BX, BX + i % BX, :, :]
        xe_head[0, i, wide, :] = start
        rhs[i] = start + first[i // BX, 2 * BX + i % BX, :, :]
    relax(rhs, 0, (HEAD, xe_head, xo_head))
    got_head1 = exchange_field(3, xe_head, 26, (4,))

    arrive(got_second)
    arrive((got_far, None))

    def spreading(i):
        if 0 <= i < ROWS:
            return second[i // BX, i % BX, :, :]
        beyond = far_x[0 if i < 0 else 1]
        return jnp.concatenate([beyond[:HALO], beyond, beyond[:HALO]], axis=0)

    coefficients(SOLUTE, spreading, True)
    for i in range(ROWS):
        lam_even[0, 0, i, wide, :] = second[i // BX, BX + i % BX, :, :] * inv[SOLUTE, i]
    retrace((SOLUTE, 0))
    moved[7].arrive()
    for r in range(BX):
        bar = right_bar(0, r)
        lam_even[1, 0, OX + r, own_y, :] = (head_weight_in[r] + coupling_rate * bar) * inv[
            HEAD, OX + r, own, :
        ]
        lam_even[2, 0, OX + r, own_y, :] = (
            lam_even[0, 4, OX + r, own_y, :] + bar * inv[SOLUTE, OX + r, own, :]
        )
    got_lam_mid = exchange_field(4, lam_even, 30, (1, 0), (2, 0), faces=(pl.ds(1, 2), 0))
    moved[8].start()

    arrive(got_head1)
    for i in range(ROWS):
        rhs[i] = xe_head[4, i, wide, :] + first[i // BX, 2 * BX + i % BX, :, :]
    relax(rhs, 4, (HEAD, xe_head, xo_head))
    got_head2 = exchange_field(5, xe_head, 38, (8,))
    arrive(got_start)
    for i in range(ROWS):
        rhs[i] = xe_solute[0, i, wide, :] + coupling_rate * xe_head[4, i, wide, :]
    relax(rhs, 0, (SOLUTE, xe_solute, xo_solute))
    got_solute1 = exchange_field(6, xe_solute, 42, (4,))
    arrive(got_lam_mid)
    retrace((HEAD, 1), (SOLUTE, 2))
    for r in range(BX):
        bar = right_bar(1, r) + coupling_rate * right_bar(2, r)
        lam_even[3, 0, OX + r, own_y, :] = (
            lam_even[1, 4, OX + r, own_y, :] + bar * inv[HEAD, OX + r, own, :]
        )
    got_lam_h1 = exchange_field(7, lam_even, 46, (3, 0))

    gather(HEAD, xe_head, xo_head, 4, 1)
    gather_drop(HEAD, xe_head, xo_head, 4, 1)
    gather(SOLUTE, xe_solute, xo_solute, 0, 2)
    gather_drop(SOLUTE, xe_solute, xo_solute, 0, 2)

    arrive(got_head2)
    arrive(got_solute1)
    for i in range(ROWS):
        rhs[i] = xe_solute[4, i, wide, :] + coupling_rate * xe_head[8, i, wide, :]
    relax(rhs, 4, (SOLUTE, xe_solute, xo_solute))
    got_solute2 = exchange_field(8, xe_solute, None, (8,))
    stores = []

    def hand_out(source, k):
        stores.append(Move(source, fields_out.at[k], store_send.at[k], store_sem.at[k], home))
        stores[-1].start()

    hand_out(xe_head.at[8, pl.ds(OX, BX), own_y, :], 0)
    hand_out(xe_solute.at[8, pl.ds(OX, BX), own_y, :], 1)
    arrive(got_lam_h1)
    retrace((HEAD, 3))
    gather(HEAD, xe_head, xo_head, 0, 3)
    gather_drop(HEAD, xe_head, xo_head, 0, 3)
    last_drop(HEAD, xe_head, 0, 3)
    last_drop(HEAD, xe_head, 4, 1)
    last_drop(SOLUTE, xe_solute, 0, 2)
    gather(SOLUTE, xe_solute, xo_solute, 4, 0)
    gather_drop(SOLUTE, xe_solute, xo_solute, 4, 0)
    arrive(got_solute2)
    last_drop(SOLUTE, xe_solute, 4, 0)

    for move in moved[8:]:
        move.arrive()
    own_lane = lane[:BY]
    inner_top = own_lane < NZ - 1
    inner_low = own_lane > 0

    def sensitivity(field, r):
        layer = jnp.where(inner_top, acc_layer[field, r], 0.0)
        drop = acc_drop[field, r + 1, own_y, :]
        east, west = acc_drop[field, r + 2, own_y, :], acc_drop[field, r, own_y, :]
        count = north_in + south_in
        if r == BX - 1:
            east = east * east_in
        if r == 0:
            west = west * west_in
        count = count + (east_in if r == BX - 1 else 1.0) + (west_in if r == 0 else 1.0)
        count = count + jnp.where(inner_top, 1.0, 0.0) + jnp.where(inner_low, 1.0, 0.0)
        total = acc_side[field, r] + layer + down(layer) - count * drop - east - west
        total = total - acc_drop[field, r + 1, pl.ds(OY + 1, BY), :] * north_in
        total = total - acc_drop[field, r + 1, pl.ds(OY - 1, BY), :] * south_in
        total = total - jnp.where(inner_top, up(drop), 0.0) - jnp.where(inner_low, down(drop), 0.0)
        return 0.5 * total - top_of(r) * drop

    sums = [jnp.zeros((BY, NZ), jnp.float32) for _ in range(MATS)]
    for r in range(BX):
        conductivity = first[1, r, own, :]
        spread_bar = sensitivity(SOLUTE, r)
        dispersivity = second[1, r, own, :] / conductivity
        total_bar = sensitivity(HEAD, r) + dispersivity * spread_bar
        scaled = total_bar * conductivity
        grads[0, r] = scaled
        grads[1, r] = spread_bar * conductivity
        material = material_in[r]
        for m in range(MATS):
            sums[m] = sums[m] + jnp.where(material == m, scaled, 0.0)
    hand_out(grads.at[0], 2)
    hand_out(grads.at[1], 3)
    mat_row = lax.broadcasted_iota(jnp.int32, (MATS, NZ), 0)
    partial = jnp.zeros((MATS, NZ), jnp.float32)
    for m in range(MATS):
        partial = jnp.where(mat_row == m, jnp.sum(sums[m], axis=0, keepdims=True), partial)
    mat_lane = lax.broadcasted_iota(jnp.int32, (MATS, NZ), 1)
    partial = jnp.sum(partial, axis=1, keepdims=True)
    partial = jnp.sum(jnp.where(mat_row == mat_lane, partial, 0.0), axis=0, keepdims=True)

    def reduce(part, at, device_of, sends, recvs, value):
        part[at] = value
        copies = []
        for t in range(1, 16):
            copies.append(
                pltpu.make_async_remote_copy(
                    src_ref=part.at[at],
                    dst_ref=part.at[at],
                    send_sem=sends.at[t],
                    recv_sem=recvs.at[t],
                    device_id=device_of(t),
                    device_id_type=MESH,
                )
            )
            copies[-1].start()
        for t in range(1, 16):
            slot = lax.rem(at - t + 16, 16)
            pltpu.make_async_remote_copy(
                src_ref=part.at[slot],
                dst_ref=part.at[slot],
                send_sem=sends.at[t],
                recv_sem=recvs.at[t],
                device_id=device_of(t),
                device_id_type=MESH,
            ).wait_recv()
        total = part[0]
        for k in range(1, 16):
            total = total + part[k]
        return copies, total

    copies, partial = reduce(part_b, b_at, b_device, send_b, recv_b, partial)
    started += copies
    copies, partial = reduce(part_a, a_at, a_device, send_a, recv_a, partial)
    started += copies
    base = jnp.ones((1, NZ), jnp.float32)
    for m in range(MATS):
        base = jnp.where(lane[:1] == m, table_in[m], base)
    grad_table_out[...] = partial / base
    for copy in started:
        copy.wait_send()
    for store in stores:
        store.arrive()
    for move in moved + stores:
        move.wait_send()


def hand_over(fields, table, head_out, solute_out, grad_cond_out, grad_disp_out, grad_table_out):
    for k, out in enumerate((head_out, solute_out, grad_cond_out, grad_disp_out)):
        out[...] = fields[k]
    for m in range(MATS):
        grad_table_out[m] = table[0, m]


def local(*arrays):
    f32 = jnp.float32
    block = jax.ShapeDtypeStruct((BX, BY, NZ), f32)
    vmem = pl.BlockSpec(memory_space=pltpu.VMEM)
    smem = pl.BlockSpec(memory_space=pltpu.SMEM)
    anywhere = pl.BlockSpec(memory_space=pl.ANY)
    fields, table = pl.pallas_call(
        kernel,
        out_shape=(
            jax.ShapeDtypeStruct((4, BX, BY, NZ), f32),
            jax.ShapeDtypeStruct((1, NZ), f32),
        ),
        in_specs=[smem if k == 6 else anywhere for k in range(10)],
        out_specs=(anywhere, vmem),
        scratch_shapes=[
            pltpu.VMEM((BX, BY, NZ), f32),
            pltpu.VMEM((BX, BY, NZ), jnp.int32),
            pltpu.VMEM((BX, BY), jnp.int32),
            pltpu.VMEM((BX, BY, NZ), f32),
            pltpu.VMEM((2, BX, BY, NZ), f32),
            pltpu.VMEM((BX, BY, NZ), jnp.int32),
            pltpu.VMEM((BX, BY, NZ), f32),
            pltpu.VMEM((2, BX, BY, NZ), f32),
            pltpu.VMEM((BY, NZ), f32),
            pltpu.SemaphoreType.DMA((4,)),
            pltpu.SemaphoreType.DMA((4,)),
            pltpu.SemaphoreType.DMA((4,)),
            pltpu.SemaphoreType.DMA((10,)),
            pltpu.SemaphoreType.DMA((10,)),
            pltpu.VMEM((3, 3 * BX + 1, COLS, NZ), f32),
            pltpu.VMEM((3, 2 * BX, COLS, NZ), f32),
            pltpu.VMEM((2, BY, NZ), f32),
            pltpu.VMEM((2, BX, HALO, NZ), f32),
            pltpu.VMEM((4, TILES, HALO, NZ), f32),
            pltpu.VMEM((4, TILES, HALO, NZ), f32),
            pltpu.VMEM((2, ROWS, COLS, NZ), f32),
            pltpu.VMEM((2, ROWS, PAD, NZ), f32),
            pltpu.VMEM((2, ROWS, COLS, NZ), f32),
            pltpu.VMEM((2, ROWS, COLS, NZ), f32),
            pltpu.VMEM((ROWS, COLS, NZ), f32),
            pltpu.VMEM((9, ROWS, PAD, NZ), f32),
            pltpu.VMEM((8, ROWS, PAD, NZ), f32),
            pltpu.VMEM((9, ROWS, PAD, NZ), f32),
            pltpu.VMEM((8, ROWS, PAD, NZ), f32),
            pltpu.VMEM((4, 5, ROWS, PAD, NZ), f32),
            pltpu.VMEM((4, 4, ROWS, PAD, NZ), f32),
            pltpu.VMEM((2, BX, BY, NZ), f32),
            pltpu.VMEM((2, BX, BY, NZ), f32),
            pltpu.VMEM((2, BX + 2, PAD, NZ), f32),
            pltpu.VMEM((16, 1, NZ), f32),
            pltpu.VMEM((16, 1, NZ), f32),
            pltpu.SemaphoreType.DMA((9, 8)),
            pltpu.SemaphoreType.DMA((9, 8)),
            pltpu.SemaphoreType.DMA((4,)),
            pltpu.SemaphoreType.DMA((4,)),
            pltpu.SemaphoreType.DMA((16,)),
            pltpu.SemaphoreType.DMA((16,)),
            pltpu.SemaphoreType.DMA((16,)),
            pltpu.SemaphoreType.DMA((16,)),
        ],
        compiler_params=pltpu.CompilerParams(
            collective_id=0, has_side_effects=True, vmem_limit_bytes=58 << 20
        ),
        name="window",
    )(*arrays)
    return pl.pallas_call(
        hand_over,
        out_shape=(block, block, block, block, jax.ShapeDtypeStruct((MATS,), f32)),
        in_specs=[vmem, vmem],
        out_specs=(vmem,) * 4 + (smem,),
        name="hand_over",
    )(fields, table)


def solution(mesh):
    block = P("gx", "gy", None)
    return jax.shard_map(
        local,
        mesh=mesh,
        in_specs=(block, block, block, block, block, block, P(), P("gx", "gy"), block, block),
        out_specs=(block, block, block, block, P()),
        check_vma=False,
    )
```

```python
import jax
import jax.numpy as jnp
from jax import lax
from jax.experimental import pallas as pl
from jax.experimental.pallas import tpu as pltpu
from jax.sharding import PartitionSpec as P

SWEEPS = 8
MATS = 8
coupling_rate = 0.5

BX, BY, NZ, HALO = 8, 16, 128, 8
GX, GY = 32, 8
ROWS = BX + 2 * HALO
COLS = BY + 2 * HALO
PAD = COLS + 16
Y0, Y1 = 8, 8 + COLS
OX, OY = HALO, 8 + HALO
MESH = pl.DeviceIdType.MESH
DIRS = ((1, 0), (-1, 0), (0, 1), (0, -1), (1, 1), (1, -1), (-1, 1), (-1, -1))
FAR = ((2, 0), (-2, 0))
FACES, CORNERS = DIRS[:4], DIRS[4:]
TILES = 50
HEAD, SOLUTE = 0, 1


def host_of(bx, by):
    z, half = bx // 4, by // 4
    pair = lax.rem(lax.rem(bx // 2, 2) + z, 2)
    x = jnp.where(half == 0, pair, 3 - pair)
    y = jnp.where(half == 0, lax.rem(by, 4), 3 - lax.rem(by, 4))
    return (z * 4 + (x // 2) * 2 + lax.rem(bx, 2), lax.rem(x, 2) * 4 + y)


def block_of(gx, gy):
    z, x, y = gx // 4, lax.rem(gx // 2, 2) * 2 + gy // 4, lax.rem(gy, 4)
    half = x // 2
    pair = jnp.where(half == 0, x, 3 - x)
    high = lax.rem(pair + z, 2)
    return (z * 4 + high * 2 + lax.rem(gx, 2), half * 4 + jnp.where(half == 0, y, 3 - y))


def place(bx, by):
    return host_of(lax.rem(bx + GX, GX), lax.rem(by + GY, GY))


def x_part(dx):
    return {0: slice(OX, OX + BX), 1: slice(0, HALO), -1: slice(OX + BX, ROWS)}[dx]


def y_from(dy):
    return {0: (0, BY), 1: (BY - HALO, HALO), -1: (0, HALO)}[dy]


def y_into(dy):
    return {0: (HALO, BY), 1: (0, HALO), -1: (HALO + BY, HALO)}[dy]


CORNER_ROWS = {
    8: ((1, 7, 7), (2, 6, 6), (3, 5, 5), (4, None, 4)),
    9: ((1, None, 8), (2, 8, 7), (3, 7, 6), (4, 6, 5), (5, None, 4)),
}


def up(cells):
    return pltpu.roll(cells, NZ - 1, 1)


def down(cells):
    return pltpu.roll(cells, 1, 1)


def kernel(
    head_hbm,
    solute_hbm,
    source_hbm,
    log_hbm,
    disp_hbm,
    material_hbm,
    table_in,
    boundary_hbm,
    head_weight_hbm,
    solute_weight_hbm,
    fields_out,
    grad_table_out,
    log_in,
    material_in,
    boundary_in,
    head_weight_in,
    grads,
    material_home,
    disp_home,
    made,
    tops_home,
    load_sem,
    store_sem,
    store_send,
    move_send,
    move_recv,
    first,
    second,
    far_x,
    far_y,
    corner_out,
    corner_in,
    cx,
    cy,
    czu,
    inv,
    rhs,
    xe_head,
    xo_head,
    xe_solute,
    xo_solute,
    lam_even,
    lam_odd,
    acc_side,
    acc_layer,
    acc_drop,
    part_a,
    part_b,
    send_sem,
    recv_sem,
    send_far,
    recv_far,
    send_a,
    recv_a,
    send_b,
    recv_b,
):
    gx, gy = lax.axis_index("gx"), lax.axis_index("gy")
    lx, ly = block_of(gx, gy)
    host, home = host_of(gx, gy), (lx, ly)
    stays = (lx == gx) & (ly == gy)
    moves = jnp.logical_not(stays)
    neighbours = {d: place(lx + d[0], ly + d[1]) for d in (*DIRS, *FAR)}
    z_at, hi_at, core_at = gx // 4, lax.rem(gx // 2, 2), lax.rem(gx, 2)
    a_at = hi_at * 8 + gy
    b_at = z_at * 2 + core_at

    def a_device(t):
        to = lax.rem(a_at + t, 16)
        return (z_at * 4 + (to // 8) * 2 + core_at, lax.rem(to, 8))

    def b_device(t):
        to = lax.rem(b_at + t, 16)
        return ((to // 2) * 4 + hi_at * 2 + lax.rem(to, 2), gy)

    own = slice(HALO, HALO + BY)
    own_y = pl.ds(OY, BY)
    wide = pl.ds(Y0, COLS)

    def center(pack, f):
        return pack.at[1, pl.ds(f * BX, BX), pl.ds(HALO, BY), :]

    loads = []
    for source, target in (
        (boundary_hbm, boundary_in),
        (log_hbm, log_in),
        (material_hbm, material_home),
        (disp_hbm, disp_home),
    ):
        loads.append(pltpu.make_async_copy(source, target, load_sem.at[len(loads)]))
        loads[-1].start()

    barrier = pltpu.get_barrier_semaphore()
    for d in (*DIRS, *FAR):
        pl.semaphore_signal(barrier, inc=1, device_id=neighbours[d], device_id_type=MESH)
    for t in range(1, 16):
        pl.semaphore_signal(barrier, inc=1, device_id=a_device(t), device_id_type=MESH)
        pl.semaphore_signal(barrier, inc=1, device_id=b_device(t), device_id_type=MESH)

    @pl.when(moves)
    def _():
        pl.semaphore_signal(barrier, inc=1, device_id=host, device_id_type=MESH)
        pl.semaphore_signal(barrier, inc=1, device_id=home, device_id_type=MESH)

    lane = lax.broadcasted_iota(jnp.int32, (COLS, NZ), 1)
    col = lax.broadcasted_iota(jnp.int32, (COLS, NZ), 0) + (ly * BY - HALO)
    col_in = jnp.where((col >= 0) & (col < GY * BY), 1.0, 0.0)
    col_face = jnp.where((col >= 0) & (col + 1 < GY * BY), 0.5, 0.0)
    top_lane = lane == NZ - 1

    def row_in(i):
        at = lx * BX + (i - HALO)
        return jnp.where((at >= 0) & (at < GX * BX), 1.0, 0.0)

    loads[0].wait()
    kind = boundary_in[...]
    factor = jnp.where(kind == 1, 1.0, jnp.where(kind == 2, 4.0, 0.0)).astype(jnp.float32)
    diagonal_at = lax.broadcasted_iota(jnp.int32, (BY, BY), 0) == lax.broadcasted_iota(
        jnp.int32, (BY, BY), 1
    )
    tops = jnp.zeros((BY, NZ), jnp.float32)
    for r in range(BX):
        spread = jnp.broadcast_to(factor[r : r + 1, :], (BY, BY))
        column = jnp.sum(jnp.where(diagonal_at, spread, 0.0), axis=1, keepdims=True)
        tops = jnp.where(lane[:BY] == r, column, tops)
    tops_home[...] = tops
    for load in loads[1:4]:
        load.wait()
    for r in range(BX):
        material = material_home[r]
        base = jnp.zeros((BY, NZ), jnp.float32)
        for m in range(MATS):
            base = jnp.where(material == m, table_in[m], base)
        conductivity = base * jnp.exp(log_in[r])
        made[0, r] = conductivity
        made[1, r] = disp_home[r] * conductivity

    class Move:
        def __init__(self, source, target, sends, recvs, to):
            self.here = pltpu.make_async_copy(source, target, recvs)
            self.there = pltpu.make_async_remote_copy(
                src_ref=source,
                dst_ref=target,
                send_sem=sends,
                recv_sem=recvs,
                device_id=to,
                device_id_type=MESH,
            )

        def start(self):
            pl.when(stays)(self.here.start)
            pl.when(moves)(self.there.start)

        def arrive(self):
            pl.when(stays)(self.here.wait)
            pl.when(moves)(self.there.wait_recv)

        def wait_send(self):
            pl.when(moves)(self.there.wait_send)

    moved = []
    for source, target in (
        (made.at[0], center(first, 0)),
        (head_hbm, center(first, 1)),
        (source_hbm, center(first, 2)),
        (tops_home, first.at[1, 3 * BX, pl.ds(HALO, BY), :]),
        (made.at[1], center(second, 0)),
        (solute_weight_hbm, center(second, 1)),
        (solute_hbm, xe_solute.at[0, pl.ds(OX, BX), own_y, :]),
        (head_weight_hbm, head_weight_in),
        (material_hbm, material_in),
    ):
        k = len(moved)
        moved.append(Move(source, target, move_send.at[k], move_recv.at[k], host))

    pl.semaphore_wait(barrier, len(DIRS) + len(FAR) + 30 + jnp.where(stays, 0, 2))
    for move in moved[:6]:
        move.start()

    near = lax.broadcasted_iota(jnp.int32, (HALO, NZ), 0)

    def launch(event, d, source, target):
        k = DIRS.index(d)
        copy = pltpu.make_async_remote_copy(
            src_ref=source,
            dst_ref=target,
            send_sem=send_sem.at[event, k],
            recv_sem=recv_sem.at[event, k],
            device_id=neighbours[d],
            device_id_type=MESH,
        )
        copy.start()
        return copy

    def exchange(event, source_of, target_of, base, fields, extra=None):
        copies = []
        late = len(fields) == 1
        if not late:
            copies.extend(launch(event, d, source_of(d), target_of(d)) for d in FACES)
        parts = []
        for k, (dx, dy) in enumerate(CORNERS):
            at = base
            for radius, read, _ in fields:
                for d, partner, cells in CORNER_ROWS[radius]:
                    tile = read(d, dx, dy)
                    if partner is not None:
                        other = read(partner, dx, dy)
                        if dy > 0:
                            tile = jnp.where(near >= HALO - cells, tile, pltpu.roll(other, HALO - cells, 0))
                        else:
                            tile = jnp.where(near < cells, tile, pltpu.roll(other, cells, 0))
                    corner_out[k, at] = tile
                    at += 1
            if extra is not None:
                corner_out[k, at] = extra[0](dx, dy)
                at += 1
            parts.append(pl.ds(base, at - base))
        copies.extend(
            launch(event, d, corner_out.at[k, parts[k]], corner_in.at[k, parts[k]])
            for k, d in enumerate(CORNERS)
        )
        if late:
            copies.extend(launch(event, d, source_of(d), target_of(d)) for d in FACES)
        started.extend(copies)

        def lay():
            for k, (dx, dy) in enumerate(CORNERS):
                at = base
                for radius, _, write in fields:
                    for d, partner, cells in CORNER_ROWS[radius]:
                        tile = corner_in[k, at]
                        write(d, dx, dy, tile)
                        if partner is not None:
                            back = cells if dy > 0 else HALO - cells
                            write(partner, dx, dy, pltpu.roll(tile, back, 0))
                        at += 1
                if extra is not None:
                    extra[1](dx, dy, corner_in[k, at])

        return copies, lay

    def exchange_pack(event, pack, base, radii, extra=None):
        def source_of(d):
            first_col, size = y_from(d[1])
            return pack.at[1, :, pl.ds(HALO + first_col, size), :]

        def target_of(d):
            first_col, size = y_into(d[1])
            return pack.at[1 - d[0], :, pl.ds(first_col, size), :]

        def field(f, radius):
            def row(d, dx):
                return f * BX + (BX - d if dx > 0 else d - 1)

            def read(d, dx, dy):
                return pack[1, row(d, dx), pl.ds(HALO + y_from(dy)[0], HALO), :]

            def write(d, dx, dy, tile):
                pack[1 - dx, row(d, dx), pl.ds(y_into(dy)[0], HALO), :] = tile

            return radius, read, write

        fields = [field(f, radius) for f, radius in enumerate(radii)]
        if extra is not None:
            at = extra
            extra = (
                lambda dx, dy: pack[1, at, pl.ds(HALO + y_from(dy)[0], HALO), :],
                lambda dx, dy, tile: pack.__setitem__(
                    (1 - dx, at, pl.ds(y_into(dy)[0], HALO), slice(None)), tile
                ),
            )
        return exchange(event, source_of, target_of, base, fields, extra)

    def exchange_field(event, ref, base, *leads, faces=None):
        lead_all = faces or leads[0]

        def source_of(d):
            first_col, size = y_from(d[1])
            return ref.at[(*lead_all, pl.ds(OX, BX), pl.ds(OY + first_col, size), slice(None))]

        def target_of(d):
            first_col, size = y_into(d[1])
            part = x_part(d[0])
            rows = pl.ds(part.start, part.stop - part.start)
            return ref.at[(*lead_all, rows, pl.ds(Y0 + first_col, size), slice(None))]

        def field(lead):
            def read(d, dx, dy):
                row = OX + BX - d if dx > 0 else OX + d - 1
                return ref[(*lead, row, pl.ds(OY + y_from(dy)[0], HALO))]

            def write(d, dx, dy, tile):
                row = OX - d if dx > 0 else OX + BX - 1 + d
                ref[(*lead, row, pl.ds(Y0 + y_into(dy)[0], HALO))] = tile

            return HALO, read, write

        if base is None:
            copies = []
            for dx, dy in FACES:
                source, target = source_of((dx, dy)), target_of((dx, dy))
                if dx != 0:
                    edge, beyond = (OX + BX - 1, OX - 1) if dx > 0 else (OX, OX + BX)
                    source = ref.at[(*lead_all, edge, own_y, slice(None))]
                    target = ref.at[(*lead_all, beyond, own_y, slice(None))]
                copies.append(launch(event, (dx, dy), source, target))
            started.extend(copies)
            return copies, None
        return exchange(event, source_of, target_of, base, [field(lead) for lead in leads])

    def arrive(got):
        copies, lay = got
        for copy in copies:
            copy.wait_recv()
        if lay is not None:
            lay()

    def send_to(d, source, target, k):
        copy = pltpu.make_async_remote_copy(
            src_ref=source,
            dst_ref=target,
            send_sem=send_far.at[k],
            recv_sem=recv_far.at[k],
            device_id=neighbours[d],
            device_id_type=MESH,
        )
        copy.start()
        return copy

    started = []
    for move in moved[:4]:
        move.arrive()
    got_first = exchange_pack(0, first, 0, (8, 8, 8), 3 * BX)
    for move in moved[4:6]:
        move.arrive()
    got_second = exchange_pack(1, second, 13, (9, 8))
    rows = pl.ds(0, BX)
    got_far = [
        send_to((2, 0), second.at[1, BX - 1, pl.ds(HALO, BY), :], far_x.at[0], 0),
        send_to((-2, 0), second.at[1, 0, pl.ds(HALO, BY), :], far_x.at[1], 1),
        send_to((0, 1), second.at[1, rows, pl.ds(HALO, HALO), :], far_y.at[0], 2),
        send_to((0, -1), second.at[1, rows, pl.ds(BY, HALO), :], far_y.at[1], 3),
    ]
    started += got_far

    for move in moved[6:8]:
        move.start()

    at_low, at_high = col == ly * BY - HALO, col == ly * BY + BY + HALO - 1
    low_face = jnp.where(at_low & (col > 0) & (col < GY * BY), 0.5, 0.0)

    def coefficients(field, value_of, beyond):
        row = value_of(0)
        face_before = None
        if beyond:
            face_before = (value_of(-1) + row) * (0.5 * row_in(-1) * row_in(0))
        for i in range(ROWS):
            face = None
            if beyond or i + 1 < ROWS:
                ahead = value_of(i + 1)
                face = (row + ahead) * (0.5 * row_in(i) * row_in(i + 1))
                if i + 1 < ROWS:
                    cx[field, i] = face
            north = pltpu.roll(row, COLS - 1, 0)
            far = beyond and OX <= i < OX + BX
            if far:
                north = jnp.where(at_high, far_y[1, i - OX, 0:1, :], north)
            side = (row + north) * col_face
            cy[field, i, wide, :] = side
            layer = jnp.where(top_lane, 0.0, 0.5 * (row + up(row)))
            czu[field, i] = layer
            under = down(layer)
            if face is not None and face_before is not None:
                south = pltpu.roll(side, 1, 0)
                if far:
                    low = (row + far_y[0, i - OX, HALO - 1 : HALO, :]) * low_face
                    south = jnp.where(at_low, low, south)
                tile = first[i // BX, 3 * BX, :, :]
                top = jnp.where(top_lane, pltpu.roll(tile, NZ - 1 - i % BX, 1), 0.0)
                diag = 1.0 + face + face_before + side + south + layer + under + top * row
                inv[field, i] = (col_in * row_in(i)) / diag
            if face is not None:
                row, face_before = ahead, face

    def sweep(field, cur, nxt, lo, hi, right, y_at=0, y_size=COLS):
        here, span = pl.ds(Y0 + y_at, y_size), pl.ds(y_at, y_size)
        ahead, behind = pl.ds(Y0 + y_at + 1, y_size), pl.ds(Y0 + y_at - 1, y_size)
        west, mid = cur[lo - 1, here, :], cur[lo, here, :]
        face_west = cx[field, lo - 1, span, :]
        for i in range(lo, hi):
            east = cur[i + 1, here, :]
            face_east = cx[field, i, span, :]
            total = face_east * east + face_west * west
            total = total + cy[field, i, here, :] * cur[i, ahead, :]
            total = total + cy[field, i, behind, :] * cur[i, behind, :]
            layer = czu[field, i, span, :]
            total = total + layer * up(mid) + down(layer * mid)
            if right is not None:
                total = total + right[i, span, :]
            nxt[i, here, :] = total * inv[field, i, span, :]
            west, mid, face_west = mid, east, face_east

    def relax(right, base, *chains):
        def step(t, upward, lo, hi, *y):
            for field, even, odd in chains:
                if upward:
                    sweep(field, even.at[t], odd.at[t], lo, hi, right, *y)
                else:
                    sweep(field, odd.at[t], even.at[t + 1], lo, hi, right, *y)

        step(base, True, 1, ROWS - 1)
        step(base, False, 2, ROWS - 2)
        step(base + 1, True, 3, ROWS - 3)
        step(base + 1, False, 4, ROWS - 4)
        step(base + 2, True, 5, ROWS - 5)
        step(base + 2, False, 6, ROWS - 6)
        step(base + 3, True, 7, ROWS - 7)
        step(base + 3, False, OX, OX + BX, HALO, BY)

    def top_of(r):
        tile = first[1, 3 * BX, own, :]
        return jnp.where(lane[:BY] == NZ - 1, pltpu.roll(tile, NZ - 1 - r, 1), 0.0)

    def retrace(*pairs):
        relax(None, 0, *((field, lam_even.at[which], lam_odd.at[which]) for field, which in pairs))

    def right_bar(which, r):
        total = lam_even[which, 0, OX + r, own_y, :] + lam_odd[which, 0, OX + r, own_y, :]
        for k in range(1, 4):
            total = total + lam_even[which, k, OX + r, own_y, :]
            total = total + lam_odd[which, k, OX + r, own_y, :]
        return total

    acc_side[...] = jnp.zeros_like(acc_side)
    acc_layer[...] = jnp.zeros_like(acc_layer)
    acc_drop[...] = jnp.zeros_like(acc_drop)
    north_in = jnp.where(col[own] + 1 < GY * BY, 1.0, 0.0)
    south_in = jnp.where(col[own] > 0, 1.0, 0.0)
    east_in, west_in = row_in(OX + BX), row_in(OX - 1)

    def around(ref, lead, r):
        east, west = ref[(*lead, r + 1, own_y)], ref[(*lead, r - 1, own_y)]
        if r == OX + BX - 1:
            east = east * east_in
        if r == OX:
            west = west * west_in
        north = ref[(*lead, r, pl.ds(OY + 1, BY))] * north_in
        south = ref[(*lead, r, pl.ds(OY - 1, BY))] * south_in
        return east + west + north + south

    def gather(field, even, odd, base, which):
        def body(t, carry):
            steps = (
                ((lam_odd, (which, 3 - t)), (even, (base + t,))),
                ((lam_even, (which, 3 - t)), (odd, (base + t,))),
            )
            for r in range(OX, OX + BX):
                side = acc_side[field, r - OX]
                layer = acc_layer[field, r - OX]
                for (lam, at), (old, old_at) in steps:
                    lam_here = lam[(*at, r, own_y)]
                    old_here = old[(*old_at, r, own_y)]
                    side = side + lam_here * around(old, old_at, r)
                    side = side + old_here * around(lam, at, r)
                    layer = layer + lam_here * up(old_here) + old_here * up(lam_here)
                acc_side[field, r - OX] = side
                acc_layer[field, r - OX] = layer
            return carry

        lax.fori_loop(0, 4, body, 0)

    def drops(field, *products):
        for r in range(OX - 1, OX + BX + 1):
            drop = acc_drop[field, r - OX + 1, wide, :]
            for (lam, at), (new, new_at) in products:
                drop = drop + lam[(*at, r, wide)] * new[(*new_at, r, wide)]
            acc_drop[field, r - OX + 1, wide, :] = drop

    def last_drop(field, even, base, which):
        drops(field, ((lam_even, (which, 0)), (even, (base + 4,))))

    def gather_drop(field, even, odd, base, which):
        def body(t, carry):
            drops(
                field,
                ((lam_odd, (which, 3 - t)), (odd, (base + t,))),
                ((lam_even, (which, 3 - t)), (even, (base + t + 1,))),
            )
            return carry

        lax.fori_loop(0, 3, body, 0)
        drops(field, ((lam_odd, (which, 0)), (odd, (base + 3,))))

    moved[6].arrive()
    got_start = exchange_field(2, xe_solute, 22, (0,))
    arrive(got_first)
    coefficients(HEAD, lambda i: first[i // BX, i % BX, :, :], False)
    for i in range(ROWS):
        start = first[i // BX, BX + i % BX, :, :]
        xe_head[0, i, wide, :] = start
        rhs[i] = start + first[i // BX, 2 * BX + i % BX, :, :]
    relax(rhs, 0, (HEAD, xe_head, xo_head))
    got_head1 = exchange_field(3, xe_head, 26, (4,))

    arrive(got_second)
    arrive((got_far, None))

    def spreading(i):
        if 0 <= i < ROWS:
            return second[i // BX, i % BX, :, :]
        beyond = far_x[0 if i < 0 else 1]
        return jnp.concatenate([beyond[:HALO], beyond, beyond[:HALO]], axis=0)

    coefficients(SOLUTE, spreading, True)
    for i in range(ROWS):
        lam_even[0, 0, i, wide, :] = second[i // BX, BX + i % BX, :, :] * inv[SOLUTE, i]
    retrace((SOLUTE, 0))
    moved[7].arrive()
    for r in range(BX):
        bar = right_bar(0, r)
        lam_even[1, 0, OX + r, own_y, :] = (head_weight_in[r] + coupling_rate * bar) * inv[
            HEAD, OX + r, own, :
        ]
        lam_even[2, 0, OX + r, own_y, :] = (
            lam_even[0, 4, OX + r, own_y, :] + bar * inv[SOLUTE, OX + r, own, :]
        )
    got_lam_mid = exchange_field(4, lam_even, 30, (1, 0), (2, 0), faces=(pl.ds(1, 2), 0))
    moved[8].start()

    arrive(got_head1)
    for i in range(ROWS):
        rhs[i] = xe_head[4, i, wide, :] + first[i // BX, 2 * BX + i % BX, :, :]
    relax(rhs, 4, (HEAD, xe_head, xo_head))
    got_head2 = exchange_field(5, xe_head, 38, (8,))
    arrive(got_start)
    for i in range(ROWS):
        rhs[i] = xe_solute[0, i, wide, :] + coupling_rate * xe_head[4, i, wide, :]
    relax(rhs, 0, (SOLUTE, xe_solute, xo_solute))
    got_solute1 = exchange_field(6, xe_solute, 42, (4,))
    arrive(got_lam_mid)
    retrace((HEAD, 1), (SOLUTE, 2))
    for r in range(BX):
        bar = right_bar(1, r) + coupling_rate * right_bar(2, r)
        lam_even[3, 0, OX + r, own_y, :] = (
            lam_even[1, 4, OX + r, own_y, :] + bar * inv[HEAD, OX + r, own, :]
        )
    got_lam_h1 = exchange_field(7, lam_even, 46, (3, 0))

    gather(HEAD, xe_head, xo_head, 4, 1)
    gather_drop(HEAD, xe_head, xo_head, 4, 1)
    gather(SOLUTE, xe_solute, xo_solute, 0, 2)
    gather_drop(SOLUTE, xe_solute, xo_solute, 0, 2)

    arrive(got_head2)
    arrive(got_solute1)
    for i in range(ROWS):
        rhs[i] = xe_solute[4, i, wide, :] + coupling_rate * xe_head[8, i, wide, :]
    relax(rhs, 4, (SOLUTE, xe_solute, xo_solute))
    got_solute2 = exchange_field(8, xe_solute, None, (8,))
    stores = []

    def hand_out(source, k):
        stores.append(Move(source, fields_out.at[k], store_send.at[k], store_sem.at[k], home))
        stores[-1].start()

    arrive(got_lam_h1)
    hand_out(xe_head.at[8, pl.ds(OX, BX), own_y, :], 0)
    hand_out(xe_solute.at[8, pl.ds(OX, BX), own_y, :], 1)
    retrace((HEAD, 3))
    gather(HEAD, xe_head, xo_head, 0, 3)
    gather_drop(HEAD, xe_head, xo_head, 0, 3)
    last_drop(HEAD, xe_head, 0, 3)
    last_drop(HEAD, xe_head, 4, 1)
    last_drop(SOLUTE, xe_solute, 0, 2)
    gather(SOLUTE, xe_solute, xo_solute, 4, 0)
    gather_drop(SOLUTE, xe_solute, xo_solute, 4, 0)
    arrive(got_solute2)
    last_drop(SOLUTE, xe_solute, 4, 0)

    for move in moved[8:]:
        move.arrive()
    own_lane = lane[:BY]
    inner_top = own_lane < NZ - 1
    inner_low = own_lane > 0

    def sensitivity(field, r):
        layer = jnp.where(inner_top, acc_layer[field, r], 0.0)
        drop = acc_drop[field, r + 1, own_y, :]
        east, west = acc_drop[field, r + 2, own_y, :], acc_drop[field, r, own_y, :]
        count = north_in + south_in
        if r == BX - 1:
            east = east * east_in
        if r == 0:
            west = west * west_in
        count = count + (east_in if r == BX - 1 else 1.0) + (west_in if r == 0 else 1.0)
        count = count + jnp.where(inner_top, 1.0, 0.0) + jnp.where(inner_low, 1.0, 0.0)
        total = acc_side[field, r] + layer + down(layer) - count * drop - east - west
        total = total - acc_drop[field, r + 1, pl.ds(OY + 1, BY), :] * north_in
        total = total - acc_drop[field, r + 1, pl.ds(OY - 1, BY), :] * south_in
        total = total - jnp.where(inner_top, up(drop), 0.0) - jnp.where(inner_low, down(drop), 0.0)
        return 0.5 * total - top_of(r) * drop

    sums = [jnp.zeros((BY, NZ), jnp.float32) for _ in range(MATS)]
    for r in range(BX):
        conductivity = first[1, r, own, :]
        spread_bar = sensitivity(SOLUTE, r)
        dispersivity = second[1, r, own, :] / conductivity
        total_bar = sensitivity(HEAD, r) + dispersivity * spread_bar
        scaled = total_bar * conductivity
        grads[0, r] = scaled
        grads[1, r] = spread_bar * conductivity
        material = material_in[r]
        for m in range(MATS):
            sums[m] = sums[m] + jnp.where(material == m, scaled, 0.0)
    mat_row = lax.broadcasted_iota(jnp.int32, (MATS, NZ), 0)
    partial = jnp.zeros((MATS, NZ), jnp.float32)
    for m in range(MATS):
        partial = jnp.where(mat_row == m, jnp.sum(sums[m], axis=0, keepdims=True), partial)
    mat_lane = lax.broadcasted_iota(jnp.int32, (MATS, NZ), 1)
    partial = jnp.sum(partial, axis=1, keepdims=True)
    partial = jnp.sum(jnp.where(mat_row == mat_lane, partial, 0.0), axis=0, keepdims=True)

    def reduce(part, at, device_of, sends, recvs, value, meanwhile=None):
        part[at] = value
        copies = []
        for t in range(1, 16):
            copies.append(
                pltpu.make_async_remote_copy(
                    src_ref=part.at[at],
                    dst_ref=part.at[at],
                    send_sem=sends.at[t],
                    recv_sem=recvs.at[t],
                    device_id=device_of(t),
                    device_id_type=MESH,
                )
            )
            copies[-1].start()
        if meanwhile is not None:
            meanwhile()
        for t in range(1, 16):
            slot = lax.rem(at - t + 16, 16)
            pltpu.make_async_remote_copy(
                src_ref=part.at[slot],
                dst_ref=part.at[slot],
                send_sem=sends.at[t],
                recv_sem=recvs.at[t],
                device_id=device_of(t),
                device_id_type=MESH,
            ).wait_recv()
        total = part[0]
        for k in range(1, 16):
            total = total + part[k]
        return copies, total

    def gradients_home():
        hand_out(grads.at[0], 2)
        hand_out(grads.at[1], 3)

    copies, partial = reduce(part_b, b_at, b_device, send_b, recv_b, partial, gradients_home)
    started += copies
    copies, partial = reduce(part_a, a_at, a_device, send_a, recv_a, partial)
    started += copies
    base = jnp.ones((1, NZ), jnp.float32)
    for m in range(MATS):
        base = jnp.where(lane[:1] == m, table_in[m], base)
    grad_table_out[...] = partial / base
    for copy in started:
        copy.wait_send()
    for store in stores:
        store.arrive()
    for move in moved + stores:
        move.wait_send()


def hand_over(fields, table, head_out, solute_out, grad_cond_out, grad_disp_out, grad_table_out):
    for k, out in enumerate((head_out, solute_out, grad_cond_out, grad_disp_out)):
        out[...] = fields[k]
    for m in range(MATS):
        grad_table_out[m] = table[0, m]


def local(*arrays):
    f32 = jnp.float32
    block = jax.ShapeDtypeStruct((BX, BY, NZ), f32)
    vmem = pl.BlockSpec(memory_space=pltpu.VMEM)
    smem = pl.BlockSpec(memory_space=pltpu.SMEM)
    anywhere = pl.BlockSpec(memory_space=pl.ANY)
    fields, table = pl.pallas_call(
        kernel,
        out_shape=(
            jax.ShapeDtypeStruct((4, BX, BY, NZ), f32),
            jax.ShapeDtypeStruct((1, NZ), f32),
        ),
        in_specs=[smem if k == 6 else anywhere for k in range(10)],
        out_specs=(anywhere, vmem),
        scratch_shapes=[
            pltpu.VMEM((BX, BY, NZ), f32),
            pltpu.VMEM((BX, BY, NZ), jnp.int32),
            pltpu.VMEM((BX, BY), jnp.int32),
            pltpu.VMEM((BX, BY, NZ), f32),
            pltpu.VMEM((2, BX, BY, NZ), f32),
            pltpu.VMEM((BX, BY, NZ), jnp.int32),
            pltpu.VMEM((BX, BY, NZ), f32),
            pltpu.VMEM((2, BX, BY, NZ), f32),
            pltpu.VMEM((BY, NZ), f32),
            pltpu.SemaphoreType.DMA((4,)),
            pltpu.SemaphoreType.DMA((4,)),
            pltpu.SemaphoreType.DMA((4,)),
            pltpu.SemaphoreType.DMA((10,)),
            pltpu.SemaphoreType.DMA((10,)),
            pltpu.VMEM((3, 3 * BX + 1, COLS, NZ), f32),
            pltpu.VMEM((3, 2 * BX, COLS, NZ), f32),
            pltpu.VMEM((2, BY, NZ), f32),
            pltpu.VMEM((2, BX, HALO, NZ), f32),
            pltpu.VMEM((4, TILES, HALO, NZ), f32),
            pltpu.VMEM((4, TILES, HALO, NZ), f32),
            pltpu.VMEM((2, ROWS, COLS, NZ), f32),
            pltpu.VMEM((2, ROWS, PAD, NZ), f32),
            pltpu.VMEM((2, ROWS, COLS, NZ), f32),
            pltpu.VMEM((2, ROWS, COLS, NZ), f32),
            pltpu.VMEM((ROWS, COLS, NZ), f32),
            pltpu.VMEM((9, ROWS, PAD, NZ), f32),
            pltpu.VMEM((8, ROWS, PAD, NZ), f32),
            pltpu.VMEM((9, ROWS, PAD, NZ), f32),
            pltpu.VMEM((8, ROWS, PAD, NZ), f32),
            pltpu.VMEM((4, 5, ROWS, PAD, NZ), f32),
            pltpu.VMEM((4, 4, ROWS, PAD, NZ), f32),
            pltpu.VMEM((2, BX, BY, NZ), f32),
            pltpu.VMEM((2, BX, BY, NZ), f32),
            pltpu.VMEM((2, BX + 2, PAD, NZ), f32),
            pltpu.VMEM((16, 1, NZ), f32),
            pltpu.VMEM((16, 1, NZ), f32),
            pltpu.SemaphoreType.DMA((9, 8)),
            pltpu.SemaphoreType.DMA((9, 8)),
            pltpu.SemaphoreType.DMA((4,)),
            pltpu.SemaphoreType.DMA((4,)),
            pltpu.SemaphoreType.DMA((16,)),
            pltpu.SemaphoreType.DMA((16,)),
            pltpu.SemaphoreType.DMA((16,)),
            pltpu.SemaphoreType.DMA((16,)),
        ],
        compiler_params=pltpu.CompilerParams(
            collective_id=0, has_side_effects=True, vmem_limit_bytes=58 << 20
        ),
        name="window",
    )(*arrays)
    return pl.pallas_call(
        hand_over,
        out_shape=(block, block, block, block, jax.ShapeDtypeStruct((MATS,), f32)),
        in_specs=[vmem, vmem],
        out_specs=(vmem,) * 4 + (smem,),
        name="hand_over",
    )(fields, table)


def solution(mesh):
    block = P("gx", "gy", None)
    return jax.shard_map(
        local,
        mesh=mesh,
        in_specs=(block, block, block, block, block, block, P(), P("gx", "gy"), block, block),
        out_specs=(block, block, block, block, P()),
        check_vma=False,
    )
```
